32 devices in a mesh: seg: 4 (over y, x), grp: 8 (over z, core).
Axes of the slice: x: 2, y: 2, z: 4, core: 2. Of those that a mesh axis runs over, the one named last changes fastest.
Arguments:
- tile_tokens: bfloat16 [32768, 1536], P(('seg', 'grp')), may hold values from -6 to 6
- gate_weight: bfloat16 [1536, 2048], P(('seg', 'grp')), may hold values from -0.15625 to 0.15625
- up_weight: bfloat16 [1536, 2048], P(('seg', 'grp')), may hold values from -0.15625 to 0.15625
- down_weight: bfloat16 [2048, 1536], P(('seg', 'grp')), may hold values from -0.125 to 0.125
- proj_weight: bfloat16 [1536, 768], replicated, may hold values from -0.15625 to 0.15625
- query_weight: bfloat16 [768, 768], replicated, may hold values from -40 to 40
- key_weight: bfloat16 [768, 768], replicated, may hold values from -1 to 1
- value_weight: bfloat16 [768, 768], replicated, may hold values from -0.21875 to 0.21875
- tile_rank: int32 [32768], P(('seg', 'grp')), may hold values from 0 to 32767, as said below
- valid_count: int32 [1], replicated, may hold values from 16384 to 32767
Outputs:
- attended: bfloat16 [8, 4096, 768], P('grp', 'seg')
The draws below stay inside these ranges and needn't reach their ends.
Inputs may be any that keep to these rules, and one draw needn't show every extreme that they name: `tile_rank`: A permutation of the positions. Device with seg index s and grp index g holds tiles 1024 * (s * (number of grp devices) + g) onward and positions 4096 * g + 1024 * s onward. At most 64 tiles of one device's batch take positions in one device's block, exactly 64 for some pairs in every draw; that number depends only on the difference of the two devices' flat indices modulo the number of devices.
All inputs are finite; a program needn't handle non-finite values.
Results may differ from the reference program's by a relative error of at most 0.028.
Values may be sent and summed in bfloat16 or wider, within the bound.
A program may use at most 192 MiB of HBM per device.

```python
import math
import jax
import jax.numpy as jnp
from jax import lax

D_VIT = 1536
FF = 2048
D = 768
HEADS = 16
LOC = 512
RATE = 4
TOK_DEV = 1024
TILES = 32768
SEG_TOK = 4096
CAP = 64
N_SEG = 4
N_GRP = 8


def key_matrix(key):
    base = jax.random.fold_in(key, 11)
    return jnp.clip(jax.random.normal(base, (D, D), jnp.float32), -5.0, 5.0) / math.sqrt(D)


def draw_key_weight(key, part):
    shared = key_matrix(key)
    return shared.astype(jnp.bfloat16)


def draw_query_weight(key, part):
    key = jax.random.fold_in(key, 2)
    own = jnp.clip(jax.random.normal(key, (D, D), jnp.float32), -5.0, 5.0) * (3.0 / math.sqrt(D))
    return own.astype(jnp.bfloat16)


def draw_tile_rank(key, part):
    key = jax.random.fold_in(key, 3)
    devices = N_SEG * N_GRP
    cell_count = devices * CAP
    favored = jax.random.randint(jax.random.fold_in(key, 1), (), 0, devices)
    cell_offset = jnp.arange(cell_count, dtype=jnp.int32) // CAP
    shuffled = jax.random.permutation(jax.random.fold_in(key, 2), cell_count).astype(jnp.int32)
    cell_score = jnp.where(cell_offset == favored, 0, cell_count) + shuffled
    cell_rank = jnp.argsort(jnp.argsort(cell_score))
    chosen = cell_rank < TOK_DEV
    offset_count = jax.ops.segment_sum(chosen.astype(jnp.int32), cell_offset, num_segments=devices)
    group_end = jnp.cumsum(offset_count).astype(jnp.int32)
    bound_top = 2 ** 30 // TOK_DEV
    column_index = jnp.arange(TOK_DEV, dtype=jnp.int32)[None, :]
    source_keys = jax.random.randint(jax.random.fold_in(key, 3), (devices, TOK_DEV), 0, bound_top) * TOK_DEV + column_index
    slot_index = jnp.argsort(source_keys, axis=1).astype(jnp.int32)
    lag_index = jnp.searchsorted(group_end, slot_index, side='right').astype(jnp.int32)
    source_dev = jnp.arange(devices, dtype=jnp.int32)[:, None]
    target_dev = (source_dev - lag_index) % devices
    target_keys = jax.random.randint(jax.random.fold_in(key, 4), (devices, TOK_DEV), 0, bound_top) * TOK_DEV + column_index
    target_perm = jnp.argsort(target_keys, axis=1).astype(jnp.int32)
    within = target_perm[target_dev, slot_index]
    position = target_dev % N_GRP * (N_SEG * TOK_DEV) + target_dev // N_GRP * TOK_DEV + within
    return position.reshape(devices * TOK_DEV).astype(jnp.int32)


def block_levels(rng, extent, cuts, least, high):
    loudness = 1.0
    for dim, shards_of in cuts:
        steps = jax.random.uniform(jax.random.fold_in(jax.random.fold_in(rng, 6), dim), (shards_of,), jnp.float32, least / len(cuts), high / len(cuts))
        loudness = loudness * jnp.repeat(jnp.exp(steps), extent[dim] // shards_of).reshape((-1,) + (1,) * (len(extent) - 1 - dim))
    return loudness


def scatter_about(stream_key, shape, spread, most, split=(), kind=jnp.bfloat16):
    array = spread * jax.random.normal(stream_key, shape, jnp.float32)
    if split:
        array = array * block_levels(stream_key, shape, split, -0.22, 0.18)
    return jnp.clip(array, -most, most).astype(kind)


def setup_inputs(seed: int = 0) -> dict:
    arg_keys = jax.random.split(jax.random.key(seed), 11)
    return {
        "tile_tokens": scatter_about(arg_keys[0], (TILES, D_VIT), 1.0, 6.0, ((0, 32),)),
        "gate_weight": scatter_about(arg_keys[1], (D_VIT, FF), D_VIT ** -0.5, 0.15625, ((0, 32),)),
        "up_weight": scatter_about(arg_keys[2], (D_VIT, FF), D_VIT ** -0.5, 0.15625, ((0, 32),)),
        "down_weight": scatter_about(arg_keys[3], (FF, D_VIT), FF ** -0.5, 0.125, ((0, 32),)),
        "proj_weight": scatter_about(arg_keys[4], (D_VIT, D), D_VIT ** -0.5, 0.15625),
        "query_weight": draw_query_weight(jax.random.fold_in(arg_keys[10], 71), 0),
        "key_weight": draw_key_weight(jax.random.fold_in(arg_keys[10], 71), 0),
        "value_weight": scatter_about(arg_keys[7], (D, D), D ** -0.5, 0.21875),
        "tile_rank": draw_tile_rank(jax.random.fold_in(arg_keys[10], 71), 0),
        "valid_count": jax.random.randint(arg_keys[9], (1,), TILES // 2, TILES).astype(jnp.int32),
    }


def layer_norm(values, epsilon):
    row_mean = lax.optimization_barrier(jnp.mean(values, axis=-1, keepdims=True))
    centered = values - row_mean
    row_var = lax.optimization_barrier(jnp.mean(centered * centered, axis=-1, keepdims=True))
    return centered * lax.rsqrt(row_var + epsilon)

def diagonal_rows(values):
    length = values.shape[0]
    shaped = values.reshape(length // RATE, RATE, HEADS // RATE, RATE, D // HEADS)
    picked = jnp.diagonal(shaped, axis1=1, axis2=3)
    return jnp.transpose(picked, (0, 1, 3, 2)).reshape(length // RATE, D)

def reference(tile_tokens, gate_weight, up_weight, down_weight, proj_weight, query_weight, key_weight, value_weight, tile_rank, valid_count):

    def tile_block(block):
        residual = block.astype(jnp.float32)
        normed = layer_norm(residual, 1e-06).astype(jnp.bfloat16)
        gate_acc = jnp.dot(normed, gate_weight, preferred_element_type=jnp.float32)
        up_acc = jnp.dot(normed, up_weight, preferred_element_type=jnp.float32)
        hidden = (jax.nn.silu(gate_acc) * up_acc).astype(jnp.bfloat16)
        mixed = residual + jnp.dot(hidden, down_weight, preferred_element_type=jnp.float32)
        final_normed = layer_norm(mixed, 1e-06).astype(jnp.bfloat16)
        return jnp.dot(final_normed, proj_weight, preferred_element_type=jnp.float32).astype(jnp.bfloat16)
    embedded = lax.map(tile_block, tile_tokens.reshape(TILES // TOK_DEV, TOK_DEV, D_VIT)).reshape(TILES, D)
    sequence = jnp.zeros((TILES, D), jnp.bfloat16).at[tile_rank.astype(jnp.int32)].set(embedded)
    live_mask = jnp.arange(TILES, dtype=jnp.int32) < valid_count[0].astype(jnp.int32)
    normed_seq = layer_norm(sequence.astype(jnp.float32), 1e-05).astype(jnp.bfloat16)
    query_rows = jnp.dot(normed_seq, query_weight, preferred_element_type=jnp.float32).astype(jnp.bfloat16)
    key_rows = jnp.dot(normed_seq, key_weight, preferred_element_type=jnp.float32).astype(jnp.bfloat16)
    value_rows = jnp.dot(normed_seq, value_weight, preferred_element_type=jnp.float32).astype(jnp.bfloat16)
    head_size = D // HEADS
    score_scale = 1.0 / math.sqrt(head_size)

    def local_branch(operands):
        query_blk, key_blk, value_blk, keep_blk = operands
        scores = jnp.einsum('qhd,khd->hqk', query_blk.astype(jnp.float32), key_blk.astype(jnp.float32), precision=lax.Precision.HIGHEST) * score_scale
        allowed = keep_blk[None, None, :] | jnp.eye(LOC, dtype=jnp.bool_)[None]
        scores = jnp.where(allowed, scores, -jnp.inf)
        row_max = lax.optimization_barrier(jnp.max(scores, axis=-1))
        weights = jnp.exp(scores - row_max[..., None])
        row_total = lax.optimization_barrier(jnp.sum(weights, axis=-1))
        rounded = lax.optimization_barrier(weights.astype(jnp.bfloat16)).astype(jnp.float32)
        accum = jnp.einsum('hqk,khd->qhd', rounded, value_blk.astype(jnp.float32), precision=lax.Precision.HIGHEST)
        return (row_max.T, row_total.T, accum)
    block_count = TILES // LOC
    near_max, near_total, near_acc = lax.map(local_branch, (query_rows.reshape(block_count, LOC, HEADS, head_size), key_rows.reshape(block_count, LOC, HEADS, head_size), value_rows.reshape(block_count, LOC, HEADS, head_size), live_mask.reshape(block_count, LOC)))
    sparse_len = SEG_TOK // RATE
    group_count = HEADS // RATE

    def dilated_branch(operands):
        query_seg, key_seg, value_seg, keep_seg = operands
        query_sp = diagonal_rows(query_seg).reshape(sparse_len, HEADS, head_size)
        key_sp = diagonal_rows(key_seg).reshape(sparse_len, HEADS, head_size)
        value_sp = diagonal_rows(value_seg).reshape(sparse_len, HEADS, head_size)
        keep_sp = jnp.tile(keep_seg.reshape(sparse_len, RATE), (1, group_count))
        scores = jnp.einsum('qhd,khd->hqk', query_sp.astype(jnp.float32), key_sp.astype(jnp.float32), precision=lax.Precision.HIGHEST) * score_scale
        allowed = keep_sp.T[:, None, :] | jnp.eye(sparse_len, dtype=jnp.bool_)[None]
        scores = jnp.where(allowed, scores, -jnp.inf)
        row_max = lax.optimization_barrier(jnp.max(scores, axis=-1))
        weights = jnp.exp(scores - row_max[..., None])
        row_total = lax.optimization_barrier(jnp.sum(weights, axis=-1))
        accum = jnp.einsum('hqk,khd->qhd', weights, value_sp.astype(jnp.float32), precision=lax.Precision.HIGHEST)
        return (row_max.T, row_total.T, accum)
    segment_count = TILES // SEG_TOK
    far_max, far_total, far_acc = lax.map(dilated_branch, (query_rows.reshape(segment_count, SEG_TOK, D), key_rows.reshape(segment_count, SEG_TOK, D), value_rows.reshape(segment_count, SEG_TOK, D), live_mask.reshape(segment_count, SEG_TOK)))
    near_shape = (TILES // RATE, RATE, group_count, RATE)
    far_shape = (TILES // RATE, 1, group_count, RATE)
    near_max = near_max.reshape(near_shape)
    near_total = near_total.reshape(near_shape)
    near_acc = near_acc.reshape(near_shape + (head_size,))
    far_max = far_max.reshape(far_shape)
    far_total = far_total.reshape(far_shape)
    far_acc = far_acc.reshape(far_shape + (head_size,))
    same_phase = jnp.eye(RATE, dtype=jnp.bool_)[:, None, :]
    best_max = jnp.where(same_phase, jnp.maximum(near_max, far_max), near_max)
    near_coef = jnp.exp(near_max - best_max)
    far_coef = jnp.where(same_phase, jnp.exp(jnp.where(same_phase, far_max - best_max, 0.0)), 0.0)
    numerator = near_coef[..., None] * near_acc + far_coef[..., None] * far_acc
    denominator = near_coef * near_total + far_coef * far_total
    attended = (numerator / denominator[..., None]).reshape(TILES, D)
    attended = jnp.where(live_mask[:, None], attended, 0.0).astype(jnp.bfloat16)
    return attended.reshape(segment_count, SEG_TOK, D)
```

```python
import math

import jax
import jax.numpy as jnp
import numpy as np
from jax import lax
from jax.experimental import pallas as pl
from jax.experimental.pallas import tpu as pltpu
from jax.sharding import PartitionSpec as P

D = 768
HEADS = 16
LOC = 512
RATE = 4
HEAD = D // HEADS
PER_PHASE = HEADS // RATE
LANES = 256
PACKED = 384
PHASE_ROWS = LOC // RATE
EXP_SCALE = math.log2(math.e) / math.sqrt(HEAD)
MASKED = -1e30
VMEM_LIMIT = 56 * 1024 * 1024


def layer_norm(values, epsilon):
    row_mean = jnp.mean(values, axis=-1, keepdims=True)
    centered = values - row_mean
    row_var = jnp.mean(centered * centered, axis=-1, keepdims=True)
    return centered * lax.rsqrt(row_var + epsilon)


def fold_rows(left, piece):
    return jnp.dot(left, piece, preferred_element_type=jnp.float32)


def lane_sources():
    key_src = np.full((RATE, LANES), -1, np.int32)
    value_src = np.full((RATE, LANES), -1, np.int32)
    for phase in range(RATE):
        for dim in range(PER_PHASE * HEAD):
            source = (dim // HEAD * RATE + phase) * HEAD + dim % HEAD
            key_src[phase, dim] = source
            value_src[phase, dim if dim < 128 else dim + 64] = source
    return key_src.reshape(1, -1), value_src.reshape(1, -1)


def key_lanes(head):
    lane = lax.broadcasted_iota(jnp.int32, (1, LANES), 1)
    return (lane >= head * HEAD) & (lane < (head + 1) * HEAD)


def value_lanes(head):
    lane = lax.broadcasted_iota(jnp.int32, (1, LANES), 1)
    dim = jnp.where(lane < 128, lane, jnp.where(lane >= 192, lane - 64, -1))
    return (dim >= head * HEAD) & (dim < (head + 1) * HEAD)


def qkv_kernel(
    rows_ref, place_ref, key_src_ref, value_src_ref, wq_ref, wk_ref, wv_ref,
    q_ref, k_ref, v_ref, kv_ref,
):
    row_count = q_ref.shape[0]
    column = lax.broadcasted_iota(jnp.int32, (D, RATE * LANES), 0)
    pick_key = (column == key_src_ref[...]).astype(jnp.bfloat16)
    pick_value = (column == value_src_ref[...]).astype(jnp.bfloat16)
    wq = fold_rows(wq_ref[...], pick_key).astype(jnp.bfloat16)
    wk = fold_rows(wk_ref[...], pick_key).astype(jnp.bfloat16)
    wv = fold_rows(wv_ref[...], pick_value).astype(jnp.bfloat16)
    place = place_ref[...]
    spare = value_src_ref[...] < 0
    for start in range(0, row_count, LOC):
        here = lax.broadcasted_iota(jnp.int32, (LOC, place.shape[1]), 0) + start
        pick = (here == place).astype(jnp.bfloat16)
        seq = fold_rows(pick, rows_ref[...])
        normed = layer_norm(seq, 1e-05).astype(jnp.bfloat16)
        block = pl.ds(start, LOC)
        q_ref[block, :] = fold_rows(normed, wq).astype(jnp.bfloat16)
        key = fold_rows(normed, wk).astype(jnp.bfloat16)
        value = jnp.where(spare, 1.0, fold_rows(normed, wv)).astype(jnp.bfloat16)
        k_ref[block, :] = key
        v_ref[block, :] = value
        low = lax.broadcasted_iota(jnp.int32, (PHASE_ROWS, 128), 1) < 64
        for phase in range(RATE):
            kp = key[phase * PHASE_ROWS:(phase + 1) * PHASE_ROWS, phase * LANES:(phase + 1) * LANES]
            vp = value[phase * PHASE_ROWS:(phase + 1) * PHASE_ROWS, phase * LANES:(phase + 1) * LANES]
            out = pl.ds(start // RATE, PHASE_ROWS)
            at = phase * PACKED
            kv_ref[out, at:at + 128] = kp[:, :128]
            kv_ref[out, at + 128:at + 256] = jnp.where(low, kp[:, 128:], vp[:, 128:])
            kv_ref[out, at + 256:at + 384] = vp[:, :128]


def near_kernel(where_ref, q_ref, k_ref, v_ref, near_ref):
    live = where_ref[0] - pl.program_id(0) * LOC
    key_row = lax.broadcasted_iota(jnp.int32, (LOC, LOC), 1)
    query_row = lax.broadcasted_iota(jnp.int32, (LOC, LOC), 0)
    key_pos = (key_row & (PHASE_ROWS - 1)) * RATE + key_row // PHASE_ROWS
    allowed = (key_pos < live) | (key_row == query_row)
    bias = jnp.where(allowed, 0.0, MASKED)
    query, key, value = q_ref[...], k_ref[...], v_ref[...]
    lane = lax.broadcasted_iota(jnp.int32, (1, LANES), 1)
    result = jnp.zeros((LOC, LANES), jnp.float32)
    for head in range(PER_PHASE):
        own = jnp.where(key_lanes(head), query, jnp.zeros_like(query))
        scores = lax.dot_general(
            own, key, (((1,), (1,)), ((), ())), preferred_element_type=jnp.float32
        ) + bias
        top = jnp.max(scores, axis=1, keepdims=True)
        weights = jnp.exp2((scores - top) * EXP_SCALE)
        acc = fold_rows(weights.astype(jnp.bfloat16), value)
        result = jnp.where(value_lanes(head) | (lane == 128 + head), acc, result)
        result = jnp.where(lane == 132 + head, top, result)
    near_ref[...] = result


def far_kernel(where_ref, value_src_ref, q_ref, near_ref, kv_ref, out_ref, att_ref, sum_ref):
    phase = pl.program_id(0)
    row_count = q_ref.shape[0]
    sparse = row_count // RATE
    key_count = kv_ref.shape[0] * kv_ref.shape[1]
    lane = lax.broadcasted_iota(jnp.int32, (1, LANES), 1)
    starts = [pl.multiple_of(base + phase * PHASE_ROWS, PHASE_ROWS) for base in range(0, row_count, LOC)]
    query = jnp.concatenate([q_ref[pl.ds(at, PHASE_ROWS), :] for at in starts], axis=0)
    near_own = jnp.concatenate([near_ref[pl.ds(at, PHASE_ROWS), :] for at in starts], axis=0)
    packed = kv_ref[...].reshape(key_count, PACKED)
    key = packed[:, :LANES]
    low = lax.broadcasted_iota(jnp.int32, (key_count, 128), 1) < 64
    middle = packed[:, 128:256]
    value = jnp.concatenate(
        [packed[:, 256:], jnp.where(low, jnp.ones_like(middle), middle)], axis=1
    )
    key_index = lax.broadcasted_iota(jnp.int32, (sparse, key_count), 1)
    query_index = lax.broadcasted_iota(jnp.int32, (sparse, key_count), 0) + where_ref[2]
    allowed = (key_index * RATE + phase < where_ref[1]) | (key_index == query_index)
    bias = jnp.where(allowed, 0.0, MASKED)
    near = near_ref[...]
    plain = jnp.zeros((row_count, LANES), jnp.float32)
    joined = jnp.zeros((sparse, LANES), jnp.float32)
    for head in range(PER_PHASE):
        own = jnp.where(key_lanes(head), query, jnp.zeros_like(query))
        scores = lax.dot_general(
            own, key, (((1,), (1,)), ((), ())), preferred_element_type=jnp.float32
        ) + bias
        top = jnp.max(scores, axis=1, keepdims=True)
        weights = jnp.exp2((scores - top) * EXP_SCALE)
        acc = fold_rows(weights.astype(jnp.bfloat16), value)
        total = acc[:, 128:129]
        near_total = near_own[:, 128 + head:129 + head]
        near_top = near_own[:, 132 + head:133 + head]
        best = jnp.maximum(top, near_top)
        near_coef = jnp.exp2((near_top - best) * EXP_SCALE)
        far_coef = jnp.exp2((top - best) * EXP_SCALE)
        merged = (near_coef * near_own + far_coef * acc) / (near_coef * near_total + far_coef * total)
        mine = value_lanes(head)
        joined = jnp.where(mine, merged, joined)
        plain = jnp.where(mine, near / near[:, 128 + head:129 + head], plain)
    att_ref[...] = plain.astype(jnp.bfloat16)
    for block, at in enumerate(starts):
        att_ref[pl.ds(at, PHASE_ROWS), :] = joined[
            block * PHASE_ROWS:(block + 1) * PHASE_ROWS
        ].astype(jnp.bfloat16)
    place = lax.broadcasted_iota(jnp.int32, (D, LANES), 0)
    spread = (place == value_src_ref[...]).astype(jnp.bfloat16)
    added = lax.dot_general(
        att_ref[...], spread, (((1,), (1,)), ((), ())), preferred_element_type=jnp.float32
    )

    @pl.when(phase == 0)
    def _():
        sum_ref[...] = added

    @pl.when(phase > 0)
    def _():
        sum_ref[...] += added

    @pl.when(phase == RATE - 1)
    def _():
        position = lax.broadcasted_iota(jnp.int32, (LOC, LOC), 0)
        row = lax.broadcasted_iota(jnp.int32, (LOC, LOC), 1)
        order = (row == (position & (RATE - 1)) * PHASE_ROWS + position // RATE).astype(jnp.bfloat16)
        for start in range(0, row_count, LOC):
            block = pl.ds(start, LOC)
            ordered = fold_rows(order, sum_ref[block, :].astype(jnp.bfloat16))
            live = lax.broadcasted_iota(jnp.int32, (LOC, 1), 0) + start < where_ref[0]
            out_ref[block, :] = jnp.where(live, ordered, 0.0).astype(jnp.bfloat16)


def attention(rows, place, query_weight, key_weight, value_weight, valid_limit, row_count):
    seg_count = lax.axis_size("seg")
    seg_here = lax.axis_index("seg")
    seg_tok = seg_count * row_count
    sparse = row_count // RATE
    seg_start = lax.axis_index("grp") * seg_tok
    where = jnp.stack([
        valid_limit - seg_start - seg_here * row_count,
        valid_limit - seg_start,
        seg_here * sparse,
    ]).astype(jnp.int32)
    key_src, value_src = (jnp.asarray(src) for src in lane_sources())
    wide = jax.ShapeDtypeStruct((row_count, RATE * LANES), jnp.bfloat16)
    params = pltpu.CompilerParams(vmem_limit_bytes=VMEM_LIMIT)
    whole = pl.BlockSpec(memory_space=pltpu.VMEM)
    scalars = pl.BlockSpec(memory_space=pltpu.SMEM)
    query, key, value, packed = pl.pallas_call(
        qkv_kernel,
        out_shape=(wide, wide, wide, jax.ShapeDtypeStruct((sparse, RATE * PACKED), jnp.bfloat16)),
        in_specs=[whole] * 7,
        out_specs=(whole,) * 4,
        compiler_params=params,
        name="qkv",
    )(rows, place, key_src, value_src, query_weight, key_weight, value_weight)
    shared = lax.all_gather(packed, "seg", axis=0)
    tile = pl.BlockSpec((LOC, LANES), lambda block, phase: (block, phase))
    near = pl.pallas_call(
        near_kernel,
        grid=(row_count // LOC, RATE),
        out_shape=jax.ShapeDtypeStruct((row_count, RATE * LANES), jnp.float32),
        in_specs=[scalars, tile, tile, tile],
        out_specs=tile,
        compiler_params=params,
        cost_estimate=pl.CostEstimate(
            flops=8 * row_count * LOC * HEADS * LANES // 2,
            bytes_accessed=20 * row_count * LANES,
            transcendentals=row_count * LOC * HEADS,
        ),
        name="near",
    )(where, query, key, value)
    tall = pl.BlockSpec((row_count, LANES), lambda phase: (0, phase))
    return pl.pallas_call(
        far_kernel,
        grid=(RATE,),
        out_shape=jax.ShapeDtypeStruct((row_count, D), jnp.bfloat16),
        in_specs=[
            scalars,
            pl.BlockSpec((1, LANES), lambda phase: (0, phase)),
            tall,
            tall,
            pl.BlockSpec((seg_count, sparse, PACKED), lambda phase: (0, 0, phase)),
        ],
        out_specs=pl.BlockSpec((row_count, D), lambda phase: (0, 0)),
        scratch_shapes=[
            pltpu.VMEM((row_count, LANES), jnp.bfloat16),
            pltpu.VMEM((row_count, D), jnp.float32),
        ],
        compiler_params=params,
        name="far",
    )(where, value_src, query, near, shared)


def feed_forward(tile_tokens, gate_weight, up_weight, down_weight, proj_weight):
    residual = tile_tokens.astype(jnp.float32)
    normed = layer_norm(residual, 1e-06).astype(jnp.bfloat16)
    gate_acc = fold_rows(normed, lax.all_gather(gate_weight, ("seg", "grp"), axis=0, tiled=True))
    up_acc = fold_rows(normed, lax.all_gather(up_weight, ("seg", "grp"), axis=0, tiled=True))
    hidden = (jax.nn.silu(gate_acc) * up_acc).astype(jnp.bfloat16)
    mixed = fold_rows(hidden, lax.all_gather(down_weight, ("seg", "grp"), axis=0, tiled=True))
    final_normed = layer_norm(residual + mixed, 1e-06).astype(jnp.bfloat16)
    return fold_rows(final_normed, proj_weight).astype(jnp.bfloat16)


def shards(
    tile_tokens,
    gate_weight,
    up_weight,
    down_weight,
    proj_weight,
    query_weight,
    key_weight,
    value_weight,
    tile_rank,
    valid_count,
):
    seg_count = lax.axis_size("seg")
    grp_count = lax.axis_size("grp")
    devices = seg_count * grp_count
    row_count = tile_tokens.shape[0]
    slot_cap = 2 * row_count // devices
    slots = devices * slot_cap
    seg_tok = seg_count * row_count
    target_grp = tile_rank // seg_tok
    target_seg = tile_rank % seg_tok // row_count
    target = target_seg * grp_count + target_grp
    within = tile_rank % row_count
    within = within // LOC * LOC + within % RATE * PHASE_ROWS + within % LOC // RATE
    onehot = target[:, None] == jnp.arange(devices, dtype=jnp.int32)[None, :]
    order = jnp.arange(row_count, dtype=jnp.int32)
    earlier = (order[None, :] < order[:, None]).astype(jnp.bfloat16)
    before = fold_rows(earlier, onehot.astype(jnp.bfloat16))
    rank_within = jnp.sum(jnp.where(onehot, before, 0.0), axis=1).astype(jnp.int32)
    slot_index = target * slot_cap + rank_within
    filled = jnp.arange(slots, dtype=jnp.int32)[:, None] == slot_index[None, :]
    send_place = jnp.sum(jnp.where(filled, within[None, :] + 1, 0), axis=1) - 1
    got_place = lax.all_to_all(
        send_place.reshape(devices, slot_cap),
        ("seg", "grp"),
        split_axis=0,
        concat_axis=0,
        tiled=True,
    ).reshape(1, slots)
    embedded = feed_forward(tile_tokens, gate_weight, up_weight, down_weight, proj_weight)
    send_rows = fold_rows(filled.astype(jnp.bfloat16), embedded).astype(jnp.bfloat16)
    got_rows = lax.all_to_all(
        send_rows.reshape(devices, slot_cap, D),
        ("seg", "grp"),
        split_axis=0,
        concat_axis=0,
        tiled=True,
    ).reshape(slots, D)
    attended = attention(
        got_rows, got_place, query_weight, key_weight, value_weight, valid_count[0], row_count
    )
    return attended[None]


def solution(mesh):
    return jax.shard_map(
        shards,
        mesh=mesh,
        in_specs=(
            P(("seg", "grp"), None),
            P(("seg", "grp"), None),
            P(("seg", "grp"), None),
            P(("seg", "grp"), None),
            P(),
            P(),
            P(),
            P(),
            P(("seg", "grp")),
            P(),
        ),
        out_specs=P("grp", "seg", None),
        check_vma=False,
    )
```

```python
import math

import jax
import jax.numpy as jnp
import numpy as np
from jax import lax
from jax.experimental import pallas as pl
from jax.experimental.pallas import tpu as pltpu
from jax.sharding import PartitionSpec as P

D = 768
HEADS = 16
LOC = 512
RATE = 4
HEAD = D // HEADS
PER_PHASE = HEADS // RATE
LANES = 256
PACKED = 384
PHASE_ROWS = LOC // RATE
EXP_SCALE = math.log2(math.e) / math.sqrt(HEAD)
MASKED = -1e30
ROW_TILE = 256
COLUMN_TILE = 512
VMEM_LIMIT = 56 * 1024 * 1024


def layer_norm(values, epsilon):
    row_mean = jnp.mean(values, axis=-1, keepdims=True)
    centered = values - row_mean
    row_var = jnp.mean(centered * centered, axis=-1, keepdims=True)
    return centered * lax.rsqrt(row_var + epsilon)


def fold_rows(left, piece):
    return jnp.dot(left, piece, preferred_element_type=jnp.float32)


def lane_sources():
    key_src = np.full((RATE, LANES), -1, np.int32)
    value_src = np.full((RATE, LANES), -1, np.int32)
    for phase in range(RATE):
        for dim in range(PER_PHASE * HEAD):
            source = (dim // HEAD * RATE + phase) * HEAD + dim % HEAD
            key_src[phase, dim] = source
            value_src[phase, dim if dim < 128 else dim + 64] = source
    return key_src.reshape(1, -1), value_src.reshape(1, -1)


def key_lanes(head):
    lane = lax.broadcasted_iota(jnp.int32, (1, LANES), 1)
    return (lane >= head * HEAD) & (lane < (head + 1) * HEAD)


def value_lanes(head):
    lane = lax.broadcasted_iota(jnp.int32, (1, LANES), 1)
    dim = jnp.where(lane < 128, lane, jnp.where(lane >= 192, lane - 64, -1))
    return (dim >= head * HEAD) & (dim < (head + 1) * HEAD)


def qkv_kernel(
    rows_ref, place_ref, key_src_ref, value_src_ref, wq_ref, wk_ref, wv_ref,
    q_ref, k_ref, v_ref, kv_ref,
):
    row_count = q_ref.shape[0]
    column = lax.broadcasted_iota(jnp.int32, (D, RATE * LANES), 0)
    pick_key = (column == key_src_ref[...]).astype(jnp.bfloat16)
    pick_value = (column == value_src_ref[...]).astype(jnp.bfloat16)
    wq = fold_rows(wq_ref[...], pick_key).astype(jnp.bfloat16)
    wk = fold_rows(wk_ref[...], pick_key).astype(jnp.bfloat16)
    wv = fold_rows(wv_ref[...], pick_value).astype(jnp.bfloat16)
    place = place_ref[...]
    spare = value_src_ref[...] < 0
    for start in range(0, row_count, LOC):
        here = lax.broadcasted_iota(jnp.int32, (LOC, place.shape[1]), 0) + start
        pick = (here == place).astype(jnp.bfloat16)
        seq = fold_rows(pick, rows_ref[...])
        normed = layer_norm(seq, 1e-05).astype(jnp.bfloat16)
        block = pl.ds(start, LOC)
        q_ref[block, :] = fold_rows(normed, wq).astype(jnp.bfloat16)
        key = fold_rows(normed, wk).astype(jnp.bfloat16)
        value = jnp.where(spare, 1.0, fold_rows(normed, wv)).astype(jnp.bfloat16)
        k_ref[block, :] = key
        v_ref[block, :] = value
        low = lax.broadcasted_iota(jnp.int32, (PHASE_ROWS, 128), 1) < 64
        for phase in range(RATE):
            kp = key[phase * PHASE_ROWS:(phase + 1) * PHASE_ROWS, phase * LANES:(phase + 1) * LANES]
            vp = value[phase * PHASE_ROWS:(phase + 1) * PHASE_ROWS, phase * LANES:(phase + 1) * LANES]
            out = pl.ds(start // RATE, PHASE_ROWS)
            at = phase * PACKED
            kv_ref[out, at:at + 128] = kp[:, :128]
            kv_ref[out, at + 128:at + 256] = jnp.where(low, kp[:, 128:], vp[:, 128:])
            kv_ref[out, at + 256:at + 384] = vp[:, :128]


def near_kernel(where_ref, q_ref, k_ref, v_ref, near_ref):
    live = where_ref[0] - pl.program_id(0) * LOC
    key_row = lax.broadcasted_iota(jnp.int32, (LOC, LOC), 1)
    query_row = lax.broadcasted_iota(jnp.int32, (LOC, LOC), 0)
    key_pos = (key_row & (PHASE_ROWS - 1)) * RATE + key_row // PHASE_ROWS
    allowed = (key_pos < live) | (key_row == query_row)
    bias = jnp.where(allowed, 0.0, MASKED)
    query, key, value = q_ref[...], k_ref[...], v_ref[...]
    lane = lax.broadcasted_iota(jnp.int32, (1, LANES), 1)
    result = jnp.zeros((LOC, LANES), jnp.float32)
    for head in range(PER_PHASE):
        own = jnp.where(key_lanes(head), query, jnp.zeros_like(query))
        scores = lax.dot_general(
            own, key, (((1,), (1,)), ((), ())), preferred_element_type=jnp.float32
        ) + bias
        top = jnp.max(scores, axis=1, keepdims=True)
        weights = jnp.exp2((scores - top) * EXP_SCALE)
        acc = fold_rows(weights.astype(jnp.bfloat16), value)
        result = jnp.where(value_lanes(head) | (lane == 128 + head), acc, result)
        result = jnp.where(lane == 132 + head, top, result)
    near_ref[...] = result


def far_kernel(where_ref, value_src_ref, q_ref, near_ref, kv_ref, out_ref, att_ref, sum_ref):
    phase = pl.program_id(0)
    row_count = q_ref.shape[0]
    sparse = row_count // RATE
    key_count = kv_ref.shape[0] * kv_ref.shape[1]
    lane = lax.broadcasted_iota(jnp.int32, (1, LANES), 1)
    starts = [pl.multiple_of(base + phase * PHASE_ROWS, PHASE_ROWS) for base in range(0, row_count, LOC)]
    query = jnp.concatenate([q_ref[pl.ds(at, PHASE_ROWS), :] for at in starts], axis=0)
    near_own = jnp.concatenate([near_ref[pl.ds(at, PHASE_ROWS), :] for at in starts], axis=0)
    packed = kv_ref[...].reshape(key_count, PACKED)
    key = packed[:, :LANES]
    low = lax.broadcasted_iota(jnp.int32, (key_count, 128), 1) < 64
    middle = packed[:, 128:256]
    value = jnp.concatenate(
        [packed[:, 256:], jnp.where(low, jnp.ones_like(middle), middle)], axis=1
    )
    key_index = lax.broadcasted_iota(jnp.int32, (sparse, key_count), 1)
    query_index = lax.broadcasted_iota(jnp.int32, (sparse, key_count), 0) + where_ref[2]
    allowed = (key_index * RATE + phase < where_ref[1]) | (key_index == query_index)
    bias = jnp.where(allowed, 0.0, MASKED)
    near = near_ref[...]
    plain = jnp.zeros((row_count, LANES), jnp.float32)
    joined = jnp.zeros((sparse, LANES), jnp.float32)
    for head in range(PER_PHASE):
        own = jnp.where(key_lanes(head), query, jnp.zeros_like(query))
        scores = lax.dot_general(
            own, key, (((1,), (1,)), ((), ())), preferred_element_type=jnp.float32
        ) + bias
        top = jnp.max(scores, axis=1, keepdims=True)
        weights = jnp.exp2((scores - top) * EXP_SCALE)
        acc = fold_rows(weights.astype(jnp.bfloat16), value)
        total = acc[:, 128:129]
        near_total = near_own[:, 128 + head:129 + head]
        near_top = near_own[:, 132 + head:133 + head]
        best = jnp.maximum(top, near_top)
        near_coef = jnp.exp2((near_top - best) * EXP_SCALE)
        far_coef = jnp.exp2((top - best) * EXP_SCALE)
        merged = (near_coef * near_own + far_coef * acc) / (near_coef * near_total + far_coef * total)
        mine = value_lanes(head)
        joined = jnp.where(mine, merged, joined)
        plain = jnp.where(mine, near / near[:, 128 + head:129 + head], plain)
    att_ref[...] = plain.astype(jnp.bfloat16)
    for block, at in enumerate(starts):
        att_ref[pl.ds(at, PHASE_ROWS), :] = joined[
            block * PHASE_ROWS:(block + 1) * PHASE_ROWS
        ].astype(jnp.bfloat16)
    place = lax.broadcasted_iota(jnp.int32, (D, LANES), 0)
    spread = (place == value_src_ref[...]).astype(jnp.bfloat16)
    added = lax.dot_general(
        att_ref[...], spread, (((1,), (1,)), ((), ())), preferred_element_type=jnp.float32
    )

    @pl.when(phase == 0)
    def _():
        sum_ref[...] = added

    @pl.when(phase > 0)
    def _():
        sum_ref[...] += added

    @pl.when(phase == RATE - 1)
    def _():
        position = lax.broadcasted_iota(jnp.int32, (LOC, LOC), 0)
        row = lax.broadcasted_iota(jnp.int32, (LOC, LOC), 1)
        order = (row == (position & (RATE - 1)) * PHASE_ROWS + position // RATE).astype(jnp.bfloat16)
        for start in range(0, row_count, LOC):
            block = pl.ds(start, LOC)
            ordered = fold_rows(order, sum_ref[block, :].astype(jnp.bfloat16))
            live = lax.broadcasted_iota(jnp.int32, (LOC, 1), 0) + start < where_ref[0]
            out_ref[block, :] = jnp.where(live, ordered, 0.0).astype(jnp.bfloat16)


def attention(rows, place, query_weight, key_weight, value_weight, valid_limit, row_count):
    seg_count = lax.axis_size("seg")
    seg_here = lax.axis_index("seg")
    seg_tok = seg_count * row_count
    sparse = row_count // RATE
    seg_start = lax.axis_index("grp") * seg_tok
    where = jnp.stack([
        valid_limit - seg_start - seg_here * row_count,
        valid_limit - seg_start,
        seg_here * sparse,
    ]).astype(jnp.int32)
    key_src, value_src = (jnp.asarray(src) for src in lane_sources())
    wide = jax.ShapeDtypeStruct((row_count, RATE * LANES), jnp.bfloat16)
    params = pltpu.CompilerParams(vmem_limit_bytes=VMEM_LIMIT)
    whole = pl.BlockSpec(memory_space=pltpu.VMEM)
    scalars = pl.BlockSpec(memory_space=pltpu.SMEM)
    query, key, value, packed = pl.pallas_call(
        qkv_kernel,
        out_shape=(wide, wide, wide, jax.ShapeDtypeStruct((sparse, RATE * PACKED), jnp.bfloat16)),
        in_specs=[whole] * 7,
        out_specs=(whole,) * 4,
        compiler_params=params,
        name="qkv",
    )(rows, place, key_src, value_src, query_weight, key_weight, value_weight)
    shared = lax.all_gather(packed, "seg", axis=0)
    tile = pl.BlockSpec((LOC, LANES), lambda block, phase: (block, phase))
    near = pl.pallas_call(
        near_kernel,
        grid=(row_count // LOC, RATE),
        out_shape=jax.ShapeDtypeStruct((row_count, RATE * LANES), jnp.float32),
        in_specs=[scalars, tile, tile, tile],
        out_specs=tile,
        compiler_params=params,
        cost_estimate=pl.CostEstimate(
            flops=8 * row_count * LOC * HEADS * LANES // 2,
            bytes_accessed=20 * row_count * LANES,
            transcendentals=row_count * LOC * HEADS,
        ),
        name="near",
    )(where, query, key, value)
    tall = pl.BlockSpec((row_count, LANES), lambda phase: (0, phase))
    return pl.pallas_call(
        far_kernel,
        grid=(RATE,),
        out_shape=jax.ShapeDtypeStruct((row_count, D), jnp.bfloat16),
        in_specs=[
            scalars,
            pl.BlockSpec((1, LANES), lambda phase: (0, phase)),
            tall,
            tall,
            pl.BlockSpec((seg_count, sparse, PACKED), lambda phase: (0, 0, phase)),
        ],
        out_specs=pl.BlockSpec((row_count, D), lambda phase: (0, 0)),
        scratch_shapes=[
            pltpu.VMEM((row_count, LANES), jnp.bfloat16),
            pltpu.VMEM((row_count, D), jnp.float32),
        ],
        compiler_params=params,
        name="far",
    )(where, value_src, query, near, shared)


def block_half(ref, rows, half):
    if half is None:
        return ref.at[rows, :]
    width = ref.shape[1] // 2
    return ref.at[rows, half * width:(half + 1) * width]


def expert_kernel(
    tokens_ref, gate_ref, up_ref, down_ref, proj_ref, slot_ref, out_ref,
    wide_ref, deep_ref, normed_ref, hidden_ref, embedded_ref, send_sem, recv_sem,
):
    seg, grp = lax.axis_index("seg"), lax.axis_index("grp")
    core, z = grp % 2, grp // 2
    seg_x = seg // 2 * 2 + 1 - seg % 2
    seg_y = (seg + 2) % 4
    seg_d = seg_y // 2 * 2 + 1 - seg_y % 2
    sibling = z * 2 + 1 - core
    gathered = (wide_ref, deep_ref)
    depth = (gate_ref.shape[0], down_ref.shape[0])
    copies = {
        "up": (0, (seg, grp + 2), None),
        "down": (9, (seg, grp - 2), None),
        "x": (1, (seg_x, grp), None),
        "y": (2, (seg_y, grp), None),
        "xy": (3, (seg_y, grp), 0),
        "yx": (4, (seg_x, grp), 1),
        "own": (5, (seg, sibling), None),
        "own_x": (6, (seg, sibling), None),
        "own_y": (7, (seg, sibling), None),
        "own_d": (8, (seg, sibling), None),
    }
    sent_block = {
        "up": seg, "down": seg, "x": seg, "y": seg, "xy": seg_x, "yx": seg_y,
        "own": seg, "own_x": seg_x, "own_y": seg_y, "own_d": seg_d,
    }
    got_block = {
        "up": seg, "x": seg_x, "y": seg_y, "xy": seg_d, "yx": seg_d,
        "own": seg, "own_x": seg_x, "own_y": seg_y, "own_d": seg_d,
    }

    def rows_of(which, block_seg, j, block_core):
        owner = block_seg * 8 + j * 2 + block_core
        return pl.ds(pl.multiple_of(owner * depth[which], 16), depth[which])

    def outgoing(which, j, kind):
        index, target, half = copies[kind]
        block = block_half(gathered[which], rows_of(which, sent_block[kind], j, core), half)
        return pltpu.make_async_remote_copy(
            src_ref=block,
            dst_ref=block,
            send_sem=send_sem.at[which, j, index],
            recv_sem=recv_sem.at[which, j, 0 if kind == "down" else index],
            device_id=target,
            device_id_type=pl.DeviceIdType.MESH,
        )

    def arrived(which, j, kind):
        index, target, half = copies[kind]
        from_core = 1 - core if kind.startswith("own") else core
        block = block_half(gathered[which], rows_of(which, got_block[kind], j, from_core), half)
        pltpu.make_async_remote_copy(
            src_ref=block,
            dst_ref=block,
            send_sem=send_sem.at[which, j, index],
            recv_sem=recv_sem.at[which, j, index],
            device_id=(seg, sibling),
            device_id_type=pl.DeviceIdType.MESH,
        ).wait_recv()

    def each_of_wave(k, do):
        if k == 0:
            do(z, True, True)
        else:
            pl.when(z >= k)(lambda: do(z - k, True, False))
            pl.when(z + k <= 3)(lambda: do(z + k, False, True))

    def enter(which, k):
        def do(j, rising, falling):
            if k > 0:
                arrived(which, j, "up")
            if rising:
                pl.when(z < 3)(lambda: outgoing(which, j, "up").start())
            if falling:
                pl.when(z > 0)(lambda: outgoing(which, j, "down").start())
            for kind in ("x", "y", "own"):
                outgoing(which, j, kind).start()
        each_of_wave(k, do)

    def cross(which, k):
        def do(j, rising, falling):
            arrived(which, j, "x")
            outgoing(which, j, "xy").start()
            outgoing(which, j, "own_x").start()
            arrived(which, j, "y")
            outgoing(which, j, "yx").start()
            outgoing(which, j, "own_y").start()
        each_of_wave(k, do)

    def close(which, k):
        def do(j, rising, falling):
            arrived(which, j, "xy")
            arrived(which, j, "yx")
            outgoing(which, j, "own_d").start()
        each_of_wave(k, do)

    def advance(which, step):
        if 0 <= step < 4:
            enter(which, step)
        if 0 <= step - 1 < 4:
            cross(which, step - 1)
        if 0 <= step - 2 < 4:
            close(which, step - 2)

    def from_sibling(which):
        for j in range(4):
            for kind in ("own", "own_x", "own_y", "own_d"):
                arrived(which, j, kind)

    barrier = pltpu.get_barrier_semaphore()

    def greet(target):
        pl.semaphore_signal(
            barrier, inc=1, device_id=target, device_id_type=pl.DeviceIdType.MESH
        )

    for target in ((seg_x, grp), (seg_y, grp), (seg, sibling)):
        greet(target)
    pl.when(z < 3)(lambda: greet((seg, grp + 2)))
    pl.when(z > 0)(lambda: greet((seg, grp - 2)))
    pl.semaphore_wait(barrier, 4 + (z + 1) // 2 % 2)

    half_width = gate_ref.shape[1]
    wide_ref[rows_of(0, seg, z, core), :half_width] = gate_ref[...]
    wide_ref[rows_of(0, seg, z, core), half_width:] = up_ref[...]
    deep_ref[rows_of(1, seg, z, core), :] = down_ref[...]
    advance(0, 0)

    row_count = tokens_ref.shape[0]

    @pl.loop(0, row_count // ROW_TILE)
    def _(tile):
        rows = pl.ds(pl.multiple_of(tile * ROW_TILE, ROW_TILE), ROW_TILE)
        normed_ref[rows, :] = layer_norm(
            tokens_ref[rows, :].astype(jnp.float32), 1e-06
        ).astype(jnp.bfloat16)

    for step in range(1, 6):
        advance(0, step)
        advance(1, step - 3)
    from_sibling(0)

    def gate_up(tile):
        rows = pl.ds(tile * ROW_TILE, ROW_TILE)

        @pl.loop(0, half_width // COLUMN_TILE)
        def _(part):
            at = pl.multiple_of(part * COLUMN_TILE, COLUMN_TILE)
            past = pl.multiple_of(part * COLUMN_TILE + half_width, COLUMN_TILE)
            normed = normed_ref[rows, :]
            gate = fold_rows(normed, wide_ref[:, pl.ds(at, COLUMN_TILE)])
            up = fold_rows(normed, wide_ref[:, pl.ds(past, COLUMN_TILE)])
            hidden_ref[rows, pl.ds(at, COLUMN_TILE)] = (
                gate / (1.0 + jnp.exp(-gate)) * up
            ).astype(jnp.bfloat16)

    tiles = row_count // ROW_TILE
    gate_up(0)
    for step in range(6, 9):
        advance(1, step - 3)
        if step - 5 < tiles:
            gate_up(step - 5)
    for tile in range(4, tiles):
        gate_up(tile)
    from_sibling(1)

    @pl.loop(0, tiles)
    def _(tile):
        rows = pl.ds(pl.multiple_of(tile * ROW_TILE, ROW_TILE), ROW_TILE)
        mixed = tokens_ref[rows, :].astype(jnp.float32) + fold_rows(
            hidden_ref[rows, :], deep_ref[...]
        )
        final = layer_norm(mixed, 1e-06).astype(jnp.bfloat16)
        embedded_ref[rows, :] = fold_rows(final, proj_ref[...]).astype(jnp.bfloat16)

    @pl.loop(0, out_ref.shape[0] // ROW_TILE)
    def _(tile):
        start = pl.multiple_of(tile * ROW_TILE, ROW_TILE)
        slot = lax.broadcasted_iota(jnp.int32, (ROW_TILE, row_count), 0) + start
        pick = (slot == slot_ref[...]).astype(jnp.bfloat16)
        out_ref[pl.ds(start, ROW_TILE), :] = fold_rows(pick, embedded_ref[...]).astype(jnp.bfloat16)

    for which in range(2):
        for j in range(4):
            for kind in copies:
                if kind == "up":
                    pl.when((z < 3) & (z >= j))(lambda: outgoing(which, j, "up").wait_send())
                elif kind == "down":
                    pl.when((z > 0) & (z <= j))(lambda: outgoing(which, j, "down").wait_send())
                else:
                    outgoing(which, j, kind).wait_send()


def gathered_send_rows(
    tile_tokens, gate_weight, up_weight, down_weight, proj_weight, slot_index, slots
):
    row_count, width = tile_tokens.shape
    hidden_width = gate_weight.shape[1]
    whole = pl.BlockSpec(memory_space=pltpu.VMEM)
    return pl.pallas_call(
        expert_kernel,
        out_shape=jax.ShapeDtypeStruct((slots, D), jnp.bfloat16),
        in_specs=[whole] * 6,
        out_specs=whole,
        scratch_shapes=[
            pltpu.VMEM((width, 2 * hidden_width), jnp.bfloat16),
            pltpu.VMEM((hidden_width, width), jnp.bfloat16),
            pltpu.VMEM((row_count, width), jnp.bfloat16),
            pltpu.VMEM((row_count, hidden_width), jnp.bfloat16),
            pltpu.VMEM((row_count, D), jnp.bfloat16),
            pltpu.SemaphoreType.DMA((2, 4, 10)),
            pltpu.SemaphoreType.DMA((2, 4, 9)),
        ],
        compiler_params=pltpu.CompilerParams(
            collective_id=0, has_side_effects=True, vmem_limit_bytes=VMEM_LIMIT
        ),
        name="feed_forward",
    )(tile_tokens, gate_weight, up_weight, down_weight, proj_weight, slot_index.reshape(1, -1))


def feed_forward(tile_tokens, gate_weight, up_weight, down_weight, proj_weight):
    residual = tile_tokens.astype(jnp.float32)
    normed = layer_norm(residual, 1e-06).astype(jnp.bfloat16)
    gate_acc = fold_rows(normed, lax.all_gather(gate_weight, ("seg", "grp"), axis=0, tiled=True))
    up_acc = fold_rows(normed, lax.all_gather(up_weight, ("seg", "grp"), axis=0, tiled=True))
    hidden = (jax.nn.silu(gate_acc) * up_acc).astype(jnp.bfloat16)
    mixed = fold_rows(hidden, lax.all_gather(down_weight, ("seg", "grp"), axis=0, tiled=True))
    final_normed = layer_norm(residual + mixed, 1e-06).astype(jnp.bfloat16)
    return fold_rows(final_normed, proj_weight).astype(jnp.bfloat16)


def shards(
    tile_tokens,
    gate_weight,
    up_weight,
    down_weight,
    proj_weight,
    query_weight,
    key_weight,
    value_weight,
    tile_rank,
    valid_count,
):
    seg_count = lax.axis_size("seg")
    grp_count = lax.axis_size("grp")
    devices = seg_count * grp_count
    row_count = tile_tokens.shape[0]
    slot_cap = 2 * row_count // devices
    slots = devices * slot_cap
    seg_tok = seg_count * row_count
    target_grp = tile_rank // seg_tok
    target_seg = tile_rank % seg_tok // row_count
    target = target_seg * grp_count + target_grp
    within = tile_rank % row_count
    within = within // LOC * LOC + within % RATE * PHASE_ROWS + within % LOC // RATE
    onehot = target[:, None] == jnp.arange(devices, dtype=jnp.int32)[None, :]
    order = jnp.arange(row_count, dtype=jnp.int32)
    earlier = (order[None, :] < order[:, None]).astype(jnp.bfloat16)
    before = fold_rows(earlier, onehot.astype(jnp.bfloat16))
    rank_within = jnp.sum(jnp.where(onehot, before, 0.0), axis=1).astype(jnp.int32)
    slot_index = target * slot_cap + rank_within
    filled = jnp.arange(slots, dtype=jnp.int32)[:, None] == slot_index[None, :]
    send_place = jnp.sum(jnp.where(filled, within[None, :] + 1, 0), axis=1) - 1
    got_place = lax.all_to_all(
        send_place.reshape(devices, slot_cap),
        ("seg", "grp"),
        split_axis=0,
        concat_axis=0,
        tiled=True,
    ).reshape(1, slots)
    if (seg_count, grp_count) == (4, 8):
        send_rows = gathered_send_rows(
            tile_tokens, gate_weight, up_weight, down_weight, proj_weight, slot_index, slots
        )
    else:
        embedded = feed_forward(tile_tokens, gate_weight, up_weight, down_weight, proj_weight)
        send_rows = fold_rows(filled.astype(jnp.bfloat16), embedded).astype(jnp.bfloat16)
    got_rows = lax.all_to_all(
        send_rows.reshape(devices, slot_cap, D),
        ("seg", "grp"),
        split_axis=0,
        concat_axis=0,
        tiled=True,
    ).reshape(slots, D)
    attended = attention(
        got_rows, got_place, query_weight, key_weight, value_weight, valid_count[0], row_count
    )
    return attended[None]


def solution(mesh):
    return jax.shard_map(
        shards,
        mesh=mesh,
        in_specs=(
            P(("seg", "grp"), None),
            P(("seg", "grp"), None),
            P(("seg", "grp"), None),
            P(("seg", "grp"), None),
            P(),
            P(),
            P(),
            P(),
            P(("seg", "grp")),
            P(),
        ),
        out_specs=P("grp", "seg", None),
        check_vma=False,
    )
```

```python
import math

import jax
import jax.numpy as jnp
import numpy as np
from jax import lax
from jax.experimental import pallas as pl
from jax.experimental.pallas import tpu as pltpu
from jax.sharding import PartitionSpec as P

D = 768
HEADS = 16
LOC = 512
RATE = 4
HEAD = D // HEADS
PER_PHASE = HEADS // RATE
LANES = 256
PACKED = 384
PHASE_ROWS = LOC // RATE
EXP_SCALE = math.log2(math.e) / math.sqrt(HEAD)
MASKED = -1e30
ROW_TILE = 256
COLUMN_TILE = 512
VMEM_LIMIT = 56 * 1024 * 1024


def layer_norm(values, epsilon):
    row_mean = jnp.mean(values, axis=-1, keepdims=True)
    centered = values - row_mean
    row_var = jnp.mean(centered * centered, axis=-1, keepdims=True)
    return centered * lax.rsqrt(row_var + epsilon)


def fold_rows(left, piece):
    return jnp.dot(left, piece, preferred_element_type=jnp.float32)


def lane_sources():
    key_src = np.full((RATE, LANES), -1, np.int32)
    value_src = np.full((RATE, LANES), -1, np.int32)
    for phase in range(RATE):
        for dim in range(PER_PHASE * HEAD):
            source = (dim // HEAD * RATE + phase) * HEAD + dim % HEAD
            key_src[phase, dim] = source
            value_src[phase, dim if dim < 128 else dim + 64] = source
    return key_src.reshape(1, -1), value_src.reshape(1, -1)


def key_lanes(head):
    lane = lax.broadcasted_iota(jnp.int32, (1, LANES), 1)
    return (lane >= head * HEAD) & (lane < (head + 1) * HEAD)


def value_lanes(head):
    lane = lax.broadcasted_iota(jnp.int32, (1, LANES), 1)
    dim = jnp.where(lane < 128, lane, jnp.where(lane >= 192, lane - 64, -1))
    return (dim >= head * HEAD) & (dim < (head + 1) * HEAD)


def pick_weights_kernel(key_src_ref, value_src_ref, wq_ref, wk_ref, wv_ref, q_ref, k_ref, v_ref):
    column = lax.broadcasted_iota(jnp.int32, (D, RATE * LANES), 0)
    pick_key = (column == key_src_ref[...]).astype(jnp.bfloat16)
    pick_value = (column == value_src_ref[...]).astype(jnp.bfloat16)
    q_ref[...] = fold_rows(wq_ref[...], pick_key).astype(jnp.bfloat16)
    k_ref[...] = fold_rows(wk_ref[...], pick_key).astype(jnp.bfloat16)
    v_ref[...] = fold_rows(wv_ref[...], pick_value).astype(jnp.bfloat16)


def key_value_block(start, rows_ref, place_ref, value_src_ref, wk_ref, wv_ref, normed_ref, k_ref, v_ref, kv_ref, kv_start):
    place = place_ref[...]
    here = lax.broadcasted_iota(jnp.int32, (LOC, place.shape[1]), 0) + start
    pick = (here == place).astype(jnp.bfloat16)
    seq = fold_rows(pick, rows_ref[...])
    normed = layer_norm(seq, 1e-05).astype(jnp.bfloat16)
    block = pl.ds(start, LOC)
    normed_ref[block, :] = normed
    key = fold_rows(normed, wk_ref[...]).astype(jnp.bfloat16)
    value = jnp.where(value_src_ref[...] < 0, 1.0, fold_rows(normed, wv_ref[...])).astype(jnp.bfloat16)
    k_ref[block, :] = key
    v_ref[block, :] = value
    low = lax.broadcasted_iota(jnp.int32, (PHASE_ROWS, 128), 1) < 64
    out = pl.ds(pl.multiple_of(kv_start + start // RATE, PHASE_ROWS), PHASE_ROWS)
    for phase in range(RATE):
        kp = key[phase * PHASE_ROWS:(phase + 1) * PHASE_ROWS, phase * LANES:(phase + 1) * LANES]
        vp = value[phase * PHASE_ROWS:(phase + 1) * PHASE_ROWS, phase * LANES:(phase + 1) * LANES]
        at = phase * PACKED
        kv_ref[out, at:at + 128] = kp[:, :128]
        kv_ref[out, at + 128:at + 256] = jnp.where(low, kp[:, 128:], vp[:, 128:])
        kv_ref[out, at + 256:at + 384] = vp[:, :128]


def qkv_kernel(
    rows_ref, place_ref, value_src_ref, wq_ref, wk_ref, wv_ref,
    q_ref, k_ref, v_ref, kv_ref, normed_ref,
):
    for start in range(0, q_ref.shape[0], LOC):
        key_value_block(
            start, rows_ref, place_ref, value_src_ref, wk_ref, wv_ref, normed_ref,
            k_ref, v_ref, kv_ref, 0,
        )
        block = pl.ds(start, LOC)
        q_ref[block, :] = fold_rows(normed_ref[block, :], wq_ref[...]).astype(jnp.bfloat16)


def near_block(live, query, key, value):
    key_row = lax.broadcasted_iota(jnp.int32, (LOC, LOC), 1)
    query_row = lax.broadcasted_iota(jnp.int32, (LOC, LOC), 0)
    key_pos = (key_row & (PHASE_ROWS - 1)) * RATE + key_row // PHASE_ROWS
    allowed = (key_pos < live) | (key_row == query_row)
    bias = jnp.where(allowed, 0.0, MASKED)
    lane = lax.broadcasted_iota(jnp.int32, (1, LANES), 1)
    result = jnp.zeros((LOC, LANES), jnp.float32)
    for head in range(PER_PHASE):
        own = jnp.where(key_lanes(head), query, jnp.zeros_like(query))
        scores = lax.dot_general(
            own, key, (((1,), (1,)), ((), ())), preferred_element_type=jnp.float32
        ) + bias
        top = jnp.max(scores, axis=1, keepdims=True)
        weights = jnp.exp2((scores - top) * EXP_SCALE)
        acc = fold_rows(weights.astype(jnp.bfloat16), value)
        result = jnp.where(value_lanes(head) | (lane == 128 + head), acc, result)
        result = jnp.where(lane == 132 + head, top, result)
    return result


def near_kernel(where_ref, q_ref, k_ref, v_ref, near_ref):
    live = where_ref[0] - pl.program_id(0) * LOC
    near_ref[...] = near_block(live, q_ref[...], k_ref[...], v_ref[...])


def far_phase(phase, where_ref, query, near_own, near, packed, value_src, att_ref, starts):
    row_count = near.shape[0]
    sparse = row_count // RATE
    key_count = packed.shape[0]
    key = packed[:, :LANES]
    low = lax.broadcasted_iota(jnp.int32, (key_count, 128), 1) < 64
    middle = packed[:, 128:256]
    value = jnp.concatenate(
        [packed[:, 256:], jnp.where(low, jnp.ones_like(middle), middle)], axis=1
    )
    key_index = lax.broadcasted_iota(jnp.int32, (sparse, key_count), 1)
    query_index = lax.broadcasted_iota(jnp.int32, (sparse, key_count), 0) + where_ref[2]
    allowed = (key_index * RATE + phase < where_ref[1]) | (key_index == query_index)
    bias = jnp.where(allowed, 0.0, MASKED)
    plain = jnp.zeros((row_count, LANES), jnp.float32)
    joined = jnp.zeros((sparse, LANES), jnp.float32)
    for head in range(PER_PHASE):
        own = jnp.where(key_lanes(head), query, jnp.zeros_like(query))
        scores = lax.dot_general(
            own, key, (((1,), (1,)), ((), ())), preferred_element_type=jnp.float32
        ) + bias
        top = jnp.max(scores, axis=1, keepdims=True)
        weights = jnp.exp2((scores - top) * EXP_SCALE)
        acc = fold_rows(weights.astype(jnp.bfloat16), value)
        total = acc[:, 128:129]
        near_total = near_own[:, 128 + head:129 + head]
        near_top = near_own[:, 132 + head:133 + head]
        best = jnp.maximum(top, near_top)
        near_coef = jnp.exp2((near_top - best) * EXP_SCALE)
        far_coef = jnp.exp2((top - best) * EXP_SCALE)
        scale = 1.0 / (near_coef * near_total + far_coef * total)
        merged = (near_coef * scale) * near_own + (far_coef * scale) * acc
        mine = value_lanes(head)
        joined = jnp.where(mine, merged, joined)
        plain = jnp.where(mine, near * (1.0 / near[:, 128 + head:129 + head]), plain)
    att_ref[...] = plain.astype(jnp.bfloat16)
    for block, at in enumerate(starts):
        att_ref[pl.ds(at, PHASE_ROWS), :] = joined[
            block * PHASE_ROWS:(block + 1) * PHASE_ROWS
        ].astype(jnp.bfloat16)
    place = lax.broadcasted_iota(jnp.int32, (D, LANES), 0)
    spread = (place == value_src).astype(jnp.bfloat16)
    return lax.dot_general(
        att_ref[...], spread, (((1,), (1,)), ((), ())), preferred_element_type=jnp.float32
    )


def phase_starts(phase, row_count):
    return [
        pl.multiple_of(base + phase * PHASE_ROWS, PHASE_ROWS) for base in range(0, row_count, LOC)
    ]


def write_ordered(where_ref, sum_ref, out_ref):
    position = lax.broadcasted_iota(jnp.int32, (LOC, LOC), 0)
    row = lax.broadcasted_iota(jnp.int32, (LOC, LOC), 1)
    order = (row == (position & (RATE - 1)) * PHASE_ROWS + position // RATE).astype(jnp.bfloat16)
    for start in range(0, out_ref.shape[0], LOC):
        block = pl.ds(start, LOC)
        ordered = fold_rows(order, sum_ref[block, :].astype(jnp.bfloat16))
        live = lax.broadcasted_iota(jnp.int32, (LOC, 1), 0) + start < where_ref[0]
        out_ref[block, :] = jnp.where(live, ordered, 0.0).astype(jnp.bfloat16)


def far_kernel(where_ref, value_src_ref, q_ref, near_ref, kv_ref, out_ref, att_ref, sum_ref):
    phase = pl.program_id(0)
    starts = phase_starts(phase, q_ref.shape[0])
    query = jnp.concatenate([q_ref[pl.ds(at, PHASE_ROWS), :] for at in starts], axis=0)
    near_own = jnp.concatenate([near_ref[pl.ds(at, PHASE_ROWS), :] for at in starts], axis=0)
    packed = kv_ref[...].reshape(kv_ref.shape[0] * kv_ref.shape[1], PACKED)
    added = far_phase(
        phase, where_ref, query, near_own, near_ref[...], packed, value_src_ref[...], att_ref, starts
    )

    @pl.when(phase == 0)
    def _():
        sum_ref[...] = added

    @pl.when(phase > 0)
    def _():
        sum_ref[...] += added

    @pl.when(phase == RATE - 1)
    def _():
        write_ordered(where_ref, sum_ref, out_ref)


def attend_kernel(
    where_ref, rows_ref, place_ref, value_src_ref, wq_ref, wk_ref, wv_ref, out_ref,
    normed_ref, q_ref, k_ref, v_ref, kv_ref, near_ref, att_ref, sum_ref, send_sem, recv_sem,
):
    seg, grp = lax.axis_index("seg"), lax.axis_index("grp")
    seg_x = seg // 2 * 2 + 1 - seg % 2
    seg_y = (seg + 2) % 4
    seg_d = seg_y // 2 * 2 + 1 - seg_y % 2
    row_count = out_ref.shape[0]
    sparse = row_count // RATE
    half = kv_ref.shape[1] // 2

    barrier = pltpu.get_barrier_semaphore()
    for target in (seg_x, seg_y):
        pl.semaphore_signal(
            barrier, inc=1, device_id=(target, grp), device_id_type=pl.DeviceIdType.MESH
        )

    def copy(index, owner, part, target):
        rows = pl.ds(pl.multiple_of(owner * sparse, sparse), sparse)
        block = kv_ref.at[rows, part * half:(part + 1) * half]
        return pltpu.make_async_remote_copy(
            src_ref=block,
            dst_ref=block,
            send_sem=send_sem.at[index],
            recv_sem=recv_sem.at[index],
            device_id=(target, grp),
            device_id_type=pl.DeviceIdType.MESH,
        )

    plan = (
        (seg, seg_x, 0, seg_x),
        (seg, seg_y, 1, seg_y),
        (seg, seg_x, 1, seg_x),
        (seg, seg_y, 0, seg_y),
        (seg_x, seg_d, 0, seg_y),
        (seg_y, seg_d, 1, seg_x),
    )

    def outgoing(index):
        sent, _, part, target = plan[index]
        return copy(index, sent, part, target)

    def arrived(index):
        _, got, part, target = plan[index]
        copy(index, got, part, target).wait_recv()

    for start in range(0, row_count, LOC):
        key_value_block(
            start, rows_ref, place_ref, value_src_ref, wk_ref, wv_ref, normed_ref,
            k_ref, v_ref, kv_ref, seg * sparse,
        )
    pl.semaphore_wait(barrier, 2)
    for index in range(4):
        outgoing(index).start()
    q_ref[...] = fold_rows(normed_ref[...], wq_ref[...]).astype(jnp.bfloat16)

    def near_rows(start):
        block = pl.ds(start, LOC)

        @pl.loop(0, RATE)
        def _(phase):
            lanes = pl.ds(pl.multiple_of(phase * LANES, LANES), LANES)
            near_ref[block, lanes] = near_block(
                where_ref[0] - start, q_ref[block, lanes], k_ref[block, lanes], v_ref[block, lanes]
            )

    near_rows(0)
    for index in (0, 1):
        arrived(index)
        outgoing(index + 4).start()
    for start in range(LOC, row_count, LOC):
        near_rows(start)
    for index in range(2, 6):
        arrived(index)
    sum_ref[...] = jnp.zeros_like(sum_ref)

    @pl.loop(0, RATE)
    def _(phase):
        lanes = pl.ds(pl.multiple_of(phase * LANES, LANES), LANES)
        starts = phase_starts(phase, row_count)
        query = jnp.concatenate([q_ref[pl.ds(at, PHASE_ROWS), lanes] for at in starts], axis=0)
        near_own = jnp.concatenate([near_ref[pl.ds(at, PHASE_ROWS), lanes] for at in starts], axis=0)
        packed = kv_ref[:, pl.ds(pl.multiple_of(phase * PACKED, PACKED), PACKED)]
        sum_ref[...] += far_phase(
            phase, where_ref, query, near_own, near_ref[:, lanes], packed,
            value_src_ref[:, lanes], att_ref, starts,
        )

    write_ordered(where_ref, sum_ref, out_ref)
    for index in range(6):
        outgoing(index).wait_send()


def attention(rows, place, query_weight, key_weight, value_weight, valid_limit, row_count):
    seg_count = lax.axis_size("seg")
    seg_here = lax.axis_index("seg")
    seg_tok = seg_count * row_count
    sparse = row_count // RATE
    seg_start = lax.axis_index("grp") * seg_tok
    where = jnp.stack([
        valid_limit - seg_start - seg_here * row_count,
        valid_limit - seg_start,
        seg_here * sparse,
    ]).astype(jnp.int32)
    key_src, value_src = (jnp.asarray(src) for src in lane_sources())
    params = pltpu.CompilerParams(vmem_limit_bytes=VMEM_LIMIT)
    whole = pl.BlockSpec(memory_space=pltpu.VMEM)
    scalars = pl.BlockSpec(memory_space=pltpu.SMEM)
    lane_weights = pl.pallas_call(
        pick_weights_kernel,
        out_shape=(jax.ShapeDtypeStruct((D, RATE * LANES), jnp.bfloat16),) * 3,
        in_specs=[whole] * 5,
        out_specs=(whole,) * 3,
        compiler_params=params,
        cost_estimate=pl.CostEstimate(
            flops=6 * D * D * RATE * LANES, bytes_accessed=14 * D * D, transcendentals=0
        ),
        name="pick_weights",
    )(key_src, value_src, query_weight, key_weight, value_weight)
    lanes = (row_count, RATE * LANES)
    wide = jax.ShapeDtypeStruct(lanes, jnp.bfloat16)
    if (seg_count, lax.axis_size("grp")) == (4, 8):
        return pl.pallas_call(
            attend_kernel,
            out_shape=jax.ShapeDtypeStruct((row_count, D), jnp.bfloat16),
            in_specs=[scalars] + [whole] * 6,
            out_specs=whole,
            scratch_shapes=[
                pltpu.VMEM((row_count, D), jnp.bfloat16),
                pltpu.VMEM(lanes, jnp.bfloat16),
                pltpu.VMEM(lanes, jnp.bfloat16),
                pltpu.VMEM(lanes, jnp.bfloat16),
                pltpu.VMEM((seg_count * sparse, RATE * PACKED), jnp.bfloat16),
                pltpu.VMEM(lanes, jnp.float32),
                pltpu.VMEM((row_count, LANES), jnp.bfloat16),
                pltpu.VMEM((row_count, D), jnp.float32),
                pltpu.SemaphoreType.DMA((6,)),
                pltpu.SemaphoreType.DMA((6,)),
            ],
            compiler_params=pltpu.CompilerParams(
                collective_id=1, has_side_effects=True, vmem_limit_bytes=VMEM_LIMIT
            ),
            name="attend",
        )(where, rows, place, value_src, *lane_weights)
    query, key, value, packed = pl.pallas_call(
        qkv_kernel,
        out_shape=(wide, wide, wide, jax.ShapeDtypeStruct((sparse, RATE * PACKED), jnp.bfloat16)),
        in_specs=[whole] * 6,
        out_specs=(whole,) * 4,
        scratch_shapes=[pltpu.VMEM((row_count, D), jnp.bfloat16)],
        compiler_params=params,
        name="qkv",
    )(rows, place, value_src, *lane_weights)
    shared = lax.all_gather(packed, "seg", axis=0)
    tile = pl.BlockSpec((LOC, LANES), lambda block, phase: (block, phase))
    near = pl.pallas_call(
        near_kernel,
        grid=(row_count // LOC, RATE),
        out_shape=jax.ShapeDtypeStruct((row_count, RATE * LANES), jnp.float32),
        in_specs=[scalars, tile, tile, tile],
        out_specs=tile,
        compiler_params=params,
        cost_estimate=pl.CostEstimate(
            flops=8 * row_count * LOC * HEADS * LANES // 2,
            bytes_accessed=20 * row_count * LANES,
            transcendentals=row_count * LOC * HEADS,
        ),
        name="near",
    )(where, query, key, value)
    tall = pl.BlockSpec((row_count, LANES), lambda phase: (0, phase))
    return pl.pallas_call(
        far_kernel,
        grid=(RATE,),
        out_shape=jax.ShapeDtypeStruct((row_count, D), jnp.bfloat16),
        in_specs=[
            scalars,
            pl.BlockSpec((1, LANES), lambda phase: (0, phase)),
            tall,
            tall,
            pl.BlockSpec((seg_count, sparse, PACKED), lambda phase: (0, 0, phase)),
        ],
        out_specs=pl.BlockSpec((row_count, D), lambda phase: (0, 0)),
        scratch_shapes=[
            pltpu.VMEM((row_count, LANES), jnp.bfloat16),
            pltpu.VMEM((row_count, D), jnp.float32),
        ],
        compiler_params=params,
        name="far",
    )(where, value_src, query, near, shared)


def block_half(ref, rows, half):
    if half is None:
        return ref.at[rows, :]
    width = ref.shape[1] // 2
    return ref.at[rows, half * width:(half + 1) * width]


def expert_kernel(
    tokens_ref, gate_ref, up_ref, down_ref, proj_ref, slot_ref, out_ref,
    wide_ref, deep_ref, normed_ref, hidden_ref, embedded_ref, send_sem, recv_sem,
):
    seg, grp = lax.axis_index("seg"), lax.axis_index("grp")
    core, z = grp % 2, grp // 2
    seg_x = seg // 2 * 2 + 1 - seg % 2
    seg_y = (seg + 2) % 4
    seg_d = seg_y // 2 * 2 + 1 - seg_y % 2
    sibling = z * 2 + 1 - core
    gathered = (wide_ref, deep_ref)
    depth = (gate_ref.shape[0], down_ref.shape[0])
    copies = {
        "up": (0, (seg, grp + 2), None),
        "down": (9, (seg, grp - 2), None),
        "x": (1, (seg_x, grp), None),
        "y": (2, (seg_y, grp), None),
        "xy": (3, (seg_y, grp), 0),
        "yx": (4, (seg_x, grp), 1),
        "own": (5, (seg, sibling), None),
        "own_x": (6, (seg, sibling), None),
        "own_y": (7, (seg, sibling), None),
        "own_d": (8, (seg, sibling), None),
    }
    sent_block = {
        "up": seg, "down": seg, "x": seg, "y": seg, "xy": seg_x, "yx": seg_y,
        "own": seg, "own_x": seg_x, "own_y": seg_y, "own_d": seg_d,
    }
    got_block = {
        "up": seg, "x": seg_x, "y": seg_y, "xy": seg_d, "yx": seg_d,
        "own": seg, "own_x": seg_x, "own_y": seg_y, "own_d": seg_d,
    }

    def rows_of(which, block_seg, j, block_core):
        owner = block_seg * 8 + j * 2 + block_core
        return pl.ds(pl.multiple_of(owner * depth[which], 16), depth[which])

    def outgoing(which, j, kind):
        index, target, half = copies[kind]
        block = block_half(gathered[which], rows_of(which, sent_block[kind], j, core), half)
        return pltpu.make_async_remote_copy(
            src_ref=block,
            dst_ref=block,
            send_sem=send_sem.at[which, j, index],
            recv_sem=recv_sem.at[which, j, 0 if kind == "down" else index],
            device_id=target,
            device_id_type=pl.DeviceIdType.MESH,
        )

    def arrived(which, j, kind):
        index, target, half = copies[kind]
        from_core = 1 - core if kind.startswith("own") else core
        block = block_half(gathered[which], rows_of(which, got_block[kind], j, from_core), half)
        pltpu.make_async_remote_copy(
            src_ref=block,
            dst_ref=block,
            send_sem=send_sem.at[which, j, index],
            recv_sem=recv_sem.at[which, j, index],
            device_id=(seg, sibling),
            device_id_type=pl.DeviceIdType.MESH,
        ).wait_recv()

    def each_of_wave(k, do):
        if k == 0:
            do(z, True, True)
        else:
            pl.when(z >= k)(lambda: do(z - k, True, False))
            pl.when(z + k <= 3)(lambda: do(z + k, False, True))

    def enter(which, k):
        def do(j, rising, falling):
            if k > 0:
                arrived(which, j, "up")
            if rising:
                pl.when(z < 3)(lambda: outgoing(which, j, "up").start())
            if falling:
                pl.when(z > 0)(lambda: outgoing(which, j, "down").start())
            for kind in ("x", "y", "own"):
                outgoing(which, j, kind).start()
        each_of_wave(k, do)

    def cross(which, k):
        def do(j, rising, falling):
            arrived(which, j, "x")
            outgoing(which, j, "xy").start()
            outgoing(which, j, "own_x").start()
            arrived(which, j, "y")
            outgoing(which, j, "yx").start()
            outgoing(which, j, "own_y").start()
        each_of_wave(k, do)

    def close(which, k):
        def do(j, rising, falling):
            arrived(which, j, "xy")
            arrived(which, j, "yx")
            outgoing(which, j, "own_d").start()
        each_of_wave(k, do)

    def advance(which, step):
        if 0 <= step < 4:
            enter(which, step)
        if 0 <= step - 1 < 4:
            cross(which, step - 1)
        if 0 <= step - 2 < 4:
            close(which, step - 2)

    def from_sibling(which):
        for j in range(4):
            for kind in ("own", "own_x", "own_y", "own_d"):
                arrived(which, j, kind)

    barrier = pltpu.get_barrier_semaphore()

    def greet(target):
        pl.semaphore_signal(
            barrier, inc=1, device_id=target, device_id_type=pl.DeviceIdType.MESH
        )

    for target in ((seg_x, grp), (seg_y, grp), (seg, sibling)):
        greet(target)
    pl.when(z < 3)(lambda: greet((seg, grp + 2)))
    pl.when(z > 0)(lambda: greet((seg, grp - 2)))
    pl.semaphore_wait(barrier, 4 + (z + 1) // 2 % 2)

    half_width = gate_ref.shape[1]
    wide_ref[rows_of(0, seg, z, core), :half_width] = gate_ref[...]
    wide_ref[rows_of(0, seg, z, core), half_width:] = up_ref[...]
    deep_ref[rows_of(1, seg, z, core), :] = down_ref[...]
    advance(0, 0)

    row_count = tokens_ref.shape[0]

    @pl.loop(0, row_count // ROW_TILE)
    def _(tile):
        rows = pl.ds(pl.multiple_of(tile * ROW_TILE, ROW_TILE), ROW_TILE)
        normed_ref[rows, :] = layer_norm(
            tokens_ref[rows, :].astype(jnp.float32), 1e-06
        ).astype(jnp.bfloat16)

    for step in range(1, 6):
        advance(0, step)
        advance(1, step - 3)
    from_sibling(0)

    def gate_up(tile):
        rows = pl.ds(tile * ROW_TILE, ROW_TILE)

        @pl.loop(0, half_width // COLUMN_TILE)
        def _(part):
            at = pl.multiple_of(part * COLUMN_TILE, COLUMN_TILE)
            past = pl.multiple_of(part * COLUMN_TILE + half_width, COLUMN_TILE)
            normed = normed_ref[rows, :]
            gate = fold_rows(normed, wide_ref[:, pl.ds(at, COLUMN_TILE)])
            up = fold_rows(normed, wide_ref[:, pl.ds(past, COLUMN_TILE)])
            hidden_ref[rows, pl.ds(at, COLUMN_TILE)] = (
                gate / (1.0 + jnp.exp(-gate)) * up
            ).astype(jnp.bfloat16)

    tiles = row_count // ROW_TILE
    gate_up(0)
    for step in range(6, 9):
        advance(1, step - 3)
        if step - 5 < tiles:
            gate_up(step - 5)
    for tile in range(4, tiles):
        gate_up(tile)
    from_sibling(1)

    @pl.loop(0, tiles)
    def _(tile):
        rows = pl.ds(pl.multiple_of(tile * ROW_TILE, ROW_TILE), ROW_TILE)
        mixed = tokens_ref[rows, :].astype(jnp.float32) + fold_rows(
            hidden_ref[rows, :], deep_ref[...]
        )
        final = layer_norm(mixed, 1e-06).astype(jnp.bfloat16)
        embedded_ref[rows, :] = fold_rows(final, proj_ref[...]).astype(jnp.bfloat16)

    @pl.loop(0, out_ref.shape[0] // ROW_TILE)
    def _(tile):
        start = pl.multiple_of(tile * ROW_TILE, ROW_TILE)
        slot = lax.broadcasted_iota(jnp.int32, (ROW_TILE, row_count), 0) + start
        pick = (slot == slot_ref[...]).astype(jnp.bfloat16)
        out_ref[pl.ds(start, ROW_TILE), :] = fold_rows(pick, embedded_ref[...]).astype(jnp.bfloat16)

    for which in range(2):
        for j in range(4):
            for kind in copies:
                if kind == "up":
                    pl.when((z < 3) & (z >= j))(lambda: outgoing(which, j, "up").wait_send())
                elif kind == "down":
                    pl.when((z > 0) & (z <= j))(lambda: outgoing(which, j, "down").wait_send())
                else:
                    outgoing(which, j, kind).wait_send()


def gathered_send_rows(
    tile_tokens, gate_weight, up_weight, down_weight, proj_weight, slot_index, slots
):
    row_count, width = tile_tokens.shape
    hidden_width = gate_weight.shape[1]
    whole = pl.BlockSpec(memory_space=pltpu.VMEM)
    return pl.pallas_call(
        expert_kernel,
        out_shape=jax.ShapeDtypeStruct((slots, D), jnp.bfloat16),
        in_specs=[whole] * 6,
        out_specs=whole,
        scratch_shapes=[
            pltpu.VMEM((width, 2 * hidden_width), jnp.bfloat16),
            pltpu.VMEM((hidden_width, width), jnp.bfloat16),
            pltpu.VMEM((row_count, width), jnp.bfloat16),
            pltpu.VMEM((row_count, hidden_width), jnp.bfloat16),
            pltpu.VMEM((row_count, D), jnp.bfloat16),
            pltpu.SemaphoreType.DMA((2, 4, 10)),
            pltpu.SemaphoreType.DMA((2, 4, 9)),
        ],
        compiler_params=pltpu.CompilerParams(
            collective_id=0, has_side_effects=True, vmem_limit_bytes=VMEM_LIMIT
        ),
        name="feed_forward",
    )(tile_tokens, gate_weight, up_weight, down_weight, proj_weight, slot_index.reshape(1, -1))


def feed_forward(tile_tokens, gate_weight, up_weight, down_weight, proj_weight):
    residual = tile_tokens.astype(jnp.float32)
    normed = layer_norm(residual, 1e-06).astype(jnp.bfloat16)
    gate_acc = fold_rows(normed, lax.all_gather(gate_weight, ("seg", "grp"), axis=0, tiled=True))
    up_acc = fold_rows(normed, lax.all_gather(up_weight, ("seg", "grp"), axis=0, tiled=True))
    hidden = (jax.nn.silu(gate_acc) * up_acc).astype(jnp.bfloat16)
    mixed = fold_rows(hidden, lax.all_gather(down_weight, ("seg", "grp"), axis=0, tiled=True))
    final_normed = layer_norm(residual + mixed, 1e-06).astype(jnp.bfloat16)
    return fold_rows(final_normed, proj_weight).astype(jnp.bfloat16)


def shards(
    tile_tokens,
    gate_weight,
    up_weight,
    down_weight,
    proj_weight,
    query_weight,
    key_weight,
    value_weight,
    tile_rank,
    valid_count,
):
    seg_count = lax.axis_size("seg")
    grp_count = lax.axis_size("grp")
    devices = seg_count * grp_count
    row_count = tile_tokens.shape[0]
    slot_cap = 2 * row_count // devices
    slots = devices * slot_cap
    seg_tok = seg_count * row_count
    target_grp = tile_rank // seg_tok
    target_seg = tile_rank % seg_tok // row_count
    target = target_seg * grp_count + target_grp
    within = tile_rank % row_count
    within = within // LOC * LOC + within % RATE * PHASE_ROWS + within % LOC // RATE
    onehot = target[:, None] == jnp.arange(devices, dtype=jnp.int32)[None, :]
    order = jnp.arange(row_count, dtype=jnp.int32)
    earlier = (order[None, :] < order[:, None]).astype(jnp.bfloat16)
    before = fold_rows(earlier, onehot.astype(jnp.bfloat16))
    rank_within = jnp.sum(jnp.where(onehot, before, 0.0), axis=1).astype(jnp.int32)
    slot_index = target * slot_cap + rank_within
    filled = jnp.arange(slots, dtype=jnp.int32)[:, None] == slot_index[None, :]
    send_place = jnp.sum(jnp.where(filled, within[None, :] + 1, 0), axis=1) - 1
    got_place = lax.all_to_all(
        send_place.reshape(devices, slot_cap),
        ("seg", "grp"),
        split_axis=0,
        concat_axis=0,
        tiled=True,
    ).reshape(1, slots)
    if (seg_count, grp_count) == (4, 8):
        send_rows = gathered_send_rows(
            tile_tokens, gate_weight, up_weight, down_weight, proj_weight, slot_index, slots
        )
    else:
        embedded = feed_forward(tile_tokens, gate_weight, up_weight, down_weight, proj_weight)
        send_rows = fold_rows(filled.astype(jnp.bfloat16), embedded).astype(jnp.bfloat16)
    got_rows = lax.all_to_all(
        send_rows.reshape(devices, slot_cap, D),
        ("seg", "grp"),
        split_axis=0,
        concat_axis=0,
        tiled=True,
    ).reshape(slots, D)
    attended = attention(
        got_rows, got_place, query_weight, key_weight, value_weight, valid_count[0], row_count
    )
    return attended[None]


def solution(mesh):
    return jax.shard_map(
        shards,
        mesh=mesh,
        in_specs=(
            P(("seg", "grp"), None),
            P(("seg", "grp"), None),
            P(("seg", "grp"), None),
            P(("seg", "grp"), None),
            P(),
            P(),
            P(),
            P(),
            P(("seg", "grp")),
            P(),
        ),
        out_specs=P("grp", "seg", None),
        check_vma=False,
    )
```

```python
import math

import jax
import jax.numpy as jnp
import numpy as np
from jax import lax
from jax.experimental import pallas as pl
from jax.experimental.pallas import tpu as pltpu
from jax.sharding import PartitionSpec as P

D = 768
HEADS = 16
LOC = 512
RATE = 4
HEAD = D // HEADS
PER_PHASE = HEADS // RATE
LANES = 256
PACKED = 384
PHASE_ROWS = LOC // RATE
EXP_SCALE = math.log2(math.e) / math.sqrt(HEAD)
MASKED = -1e30
ROW_TILE = 256
COLUMN_TILE = 512
VMEM_LIMIT = 56 * 1024 * 1024


def layer_norm(values, epsilon):
    row_mean = jnp.mean(values, axis=-1, keepdims=True)
    centered = values - row_mean
    row_var = jnp.mean(centered * centered, axis=-1, keepdims=True)
    return centered * lax.rsqrt(row_var + epsilon)


def fold_rows(left, piece):
    return jnp.dot(left, piece, preferred_element_type=jnp.float32)


def lane_sources():
    key_src = np.full((RATE, LANES), -1, np.int32)
    value_src = np.full((RATE, LANES), -1, np.int32)
    for phase in range(RATE):
        for dim in range(PER_PHASE * HEAD):
            source = (dim // HEAD * RATE + phase) * HEAD + dim % HEAD
            key_src[phase, dim] = source
            value_src[phase, dim if dim < 128 else dim + 64] = source
    return key_src.reshape(1, -1), value_src.reshape(1, -1)


def key_lanes(head):
    lane = lax.broadcasted_iota(jnp.int32, (1, LANES), 1)
    return (lane >= head * HEAD) & (lane < (head + 1) * HEAD)


def value_lanes(head):
    lane = lax.broadcasted_iota(jnp.int32, (1, LANES), 1)
    dim = jnp.where(lane < 128, lane, jnp.where(lane >= 192, lane - 64, -1))
    return (dim >= head * HEAD) & (dim < (head + 1) * HEAD)


def pick_weights_kernel(key_src_ref, value_src_ref, wq_ref, wk_ref, wv_ref, q_ref, k_ref, v_ref):
    column = lax.broadcasted_iota(jnp.int32, (D, RATE * LANES), 0)
    pick_key = (column == key_src_ref[...]).astype(jnp.bfloat16)
    pick_value = (column == value_src_ref[...]).astype(jnp.bfloat16)
    q_ref[...] = fold_rows(wq_ref[...], pick_key).astype(jnp.bfloat16)
    k_ref[...] = fold_rows(wk_ref[...], pick_key).astype(jnp.bfloat16)
    v_ref[...] = fold_rows(wv_ref[...], pick_value).astype(jnp.bfloat16)


def key_value_block(start, rows_ref, place_ref, value_src_ref, wk_ref, wv_ref, normed_ref, k_ref, v_ref, kv_ref, kv_start):
    place = place_ref[...]
    here = lax.broadcasted_iota(jnp.int32, (LOC, place.shape[1]), 0) + start
    pick = (here == place).astype(jnp.bfloat16)
    seq = fold_rows(pick, rows_ref[...])
    normed = layer_norm(seq, 1e-05).astype(jnp.bfloat16)
    block = pl.ds(start, LOC)
    normed_ref[block, :] = normed
    key = fold_rows(normed, wk_ref[...]).astype(jnp.bfloat16)
    value = jnp.where(value_src_ref[...] < 0, 1.0, fold_rows(normed, wv_ref[...])).astype(jnp.bfloat16)
    k_ref[block, :] = key
    v_ref[block, :] = value
    low = lax.broadcasted_iota(jnp.int32, (PHASE_ROWS, 128), 1) < 64
    out = pl.ds(pl.multiple_of(kv_start + start // RATE, PHASE_ROWS), PHASE_ROWS)
    for phase in range(RATE):
        kp = key[phase * PHASE_ROWS:(phase + 1) * PHASE_ROWS, phase * LANES:(phase + 1) * LANES]
        vp = value[phase * PHASE_ROWS:(phase + 1) * PHASE_ROWS, phase * LANES:(phase + 1) * LANES]
        at = phase * PACKED
        kv_ref[out, at:at + 128] = kp[:, :128]
        kv_ref[out, at + 128:at + 256] = jnp.where(low, kp[:, 128:], vp[:, 128:])
        kv_ref[out, at + 256:at + 384] = vp[:, :128]


def qkv_kernel(
    rows_ref, place_ref, value_src_ref, wq_ref, wk_ref, wv_ref,
    q_ref, k_ref, v_ref, kv_ref, normed_ref,
):
    for start in range(0, q_ref.shape[0], LOC):
        key_value_block(
            start, rows_ref, place_ref, value_src_ref, wk_ref, wv_ref, normed_ref,
            k_ref, v_ref, kv_ref, 0,
        )
        block = pl.ds(start, LOC)
        q_ref[block, :] = fold_rows(normed_ref[block, :], wq_ref[...]).astype(jnp.bfloat16)


def near_block(live, query, key, value):
    key_row = lax.broadcasted_iota(jnp.int32, (LOC, LOC), 1)
    query_row = lax.broadcasted_iota(jnp.int32, (LOC, LOC), 0)
    key_pos = (key_row & (PHASE_ROWS - 1)) * RATE + key_row // PHASE_ROWS
    allowed = (key_pos < live) | (key_row == query_row)
    bias = jnp.where(allowed, 0.0, MASKED)
    lane = lax.broadcasted_iota(jnp.int32, (1, LANES), 1)
    result = jnp.zeros((LOC, LANES), jnp.float32)
    for head in range(PER_PHASE):
        own = jnp.where(key_lanes(head), query, jnp.zeros_like(query))
        scores = lax.dot_general(
            own, key, (((1,), (1,)), ((), ())), preferred_element_type=jnp.float32
        ) + bias
        top = jnp.max(scores, axis=1, keepdims=True)
        weights = jnp.exp2((scores - top) * EXP_SCALE)
        acc = fold_rows(weights.astype(jnp.bfloat16), value)
        result = jnp.where(value_lanes(head) | (lane == 128 + head), acc, result)
        result = jnp.where(lane == 132 + head, top, result)
    return result


def near_kernel(where_ref, q_ref, k_ref, v_ref, near_ref):
    live = where_ref[0] - pl.program_id(0) * LOC
    near_ref[...] = near_block(live, q_ref[...], k_ref[...], v_ref[...])


def far_phase(phase, where_ref, query, near_own, near, packed, value_src, att_ref, starts):
    row_count = near.shape[0]
    sparse = row_count // RATE
    key_count = packed.shape[0]
    key = packed[:, :LANES]
    low = lax.broadcasted_iota(jnp.int32, (key_count, 128), 1) < 64
    middle = packed[:, 128:256]
    value = jnp.concatenate(
        [packed[:, 256:], jnp.where(low, jnp.ones_like(middle), middle)], axis=1
    )
    key_index = lax.broadcasted_iota(jnp.int32, (sparse, key_count), 1)
    query_index = lax.broadcasted_iota(jnp.int32, (sparse, key_count), 0) + where_ref[2]
    allowed = (key_index * RATE + phase < where_ref[1]) | (key_index == query_index)
    bias = jnp.where(allowed, 0.0, MASKED)
    plain = jnp.zeros((row_count, LANES), jnp.float32)
    joined = jnp.zeros((sparse, LANES), jnp.float32)
    for head in range(PER_PHASE):
        own = jnp.where(key_lanes(head), query, jnp.zeros_like(query))
        scores = lax.dot_general(
            own, key, (((1,), (1,)), ((), ())), preferred_element_type=jnp.float32
        ) + bias
        top = jnp.max(scores, axis=1, keepdims=True)
        weights = jnp.exp2((scores - top) * EXP_SCALE)
        acc = fold_rows(weights.astype(jnp.bfloat16), value)
        total = acc[:, 128:129]
        near_total = near_own[:, 128 + head:129 + head]
        near_top = near_own[:, 132 + head:133 + head]
        best = jnp.maximum(top, near_top)
        near_coef = jnp.exp2((near_top - best) * EXP_SCALE)
        far_coef = jnp.exp2((top - best) * EXP_SCALE)
        scale = 1.0 / (near_coef * near_total + far_coef * total)
        merged = (near_coef * scale) * near_own + (far_coef * scale) * acc
        mine = value_lanes(head)
        joined = jnp.where(mine, merged, joined)
        plain = jnp.where(mine, near * (1.0 / near[:, 128 + head:129 + head]), plain)
    att_ref[...] = plain.astype(jnp.bfloat16)
    for block, at in enumerate(starts):
        att_ref[pl.ds(at, PHASE_ROWS), :] = joined[
            block * PHASE_ROWS:(block + 1) * PHASE_ROWS
        ].astype(jnp.bfloat16)
    place = lax.broadcasted_iota(jnp.int32, (D, LANES), 0)
    spread = (place == value_src).astype(jnp.bfloat16)
    return lax.dot_general(
        att_ref[...], spread, (((1,), (1,)), ((), ())), preferred_element_type=jnp.float32
    )


def phase_starts(phase, row_count):
    return [
        pl.multiple_of(base + phase * PHASE_ROWS, PHASE_ROWS) for base in range(0, row_count, LOC)
    ]


def write_ordered(where_ref, sum_ref, out_ref):
    position = lax.broadcasted_iota(jnp.int32, (LOC, LOC), 0)
    row = lax.broadcasted_iota(jnp.int32, (LOC, LOC), 1)
    order = (row == (position & (RATE - 1)) * PHASE_ROWS + position // RATE).astype(jnp.bfloat16)
    for start in range(0, out_ref.shape[0], LOC):
        block = pl.ds(start, LOC)
        ordered = fold_rows(order, sum_ref[block, :].astype(jnp.bfloat16))
        live = lax.broadcasted_iota(jnp.int32, (LOC, 1), 0) + start < where_ref[0]
        out_ref[block, :] = jnp.where(live, ordered, 0.0).astype(jnp.bfloat16)


def far_kernel(where_ref, value_src_ref, q_ref, near_ref, kv_ref, out_ref, att_ref, sum_ref):
    phase = pl.program_id(0)
    starts = phase_starts(phase, q_ref.shape[0])
    query = jnp.concatenate([q_ref[pl.ds(at, PHASE_ROWS), :] for at in starts], axis=0)
    near_own = jnp.concatenate([near_ref[pl.ds(at, PHASE_ROWS), :] for at in starts], axis=0)
    packed = kv_ref[...].reshape(kv_ref.shape[0] * kv_ref.shape[1], PACKED)
    added = far_phase(
        phase, where_ref, query, near_own, near_ref[...], packed, value_src_ref[...], att_ref, starts
    )

    @pl.when(phase == 0)
    def _():
        sum_ref[...] = added

    @pl.when(phase > 0)
    def _():
        sum_ref[...] += added

    @pl.when(phase == RATE - 1)
    def _():
        write_ordered(where_ref, sum_ref, out_ref)


def attend_kernel(
    where_ref, rows_ref, place_ref, value_src_ref, wq_ref, wk_ref, wv_ref, out_ref,
    normed_ref, q_ref, k_ref, v_ref, kv_ref, near_ref, att_ref, sum_ref, send_sem, recv_sem,
):
    seg, grp = lax.axis_index("seg"), lax.axis_index("grp")
    seg_x = seg // 2 * 2 + 1 - seg % 2
    seg_y = (seg + 2) % 4
    seg_d = seg_y // 2 * 2 + 1 - seg_y % 2
    row_count = out_ref.shape[0]
    sparse = row_count // RATE
    half = kv_ref.shape[1] // 2

    barrier = pltpu.get_barrier_semaphore()
    for target in (seg_x, seg_y):
        pl.semaphore_signal(
            barrier, inc=1, device_id=(target, grp), device_id_type=pl.DeviceIdType.MESH
        )

    def copy(index, owner, part, target):
        rows = pl.ds(pl.multiple_of(owner * sparse, sparse), sparse)
        block = kv_ref.at[rows, part * half:(part + 1) * half]
        return pltpu.make_async_remote_copy(
            src_ref=block,
            dst_ref=block,
            send_sem=send_sem.at[index],
            recv_sem=recv_sem.at[index],
            device_id=(target, grp),
            device_id_type=pl.DeviceIdType.MESH,
        )

    plan = (
        (seg, seg_x, 0, seg_x),
        (seg, seg_y, 1, seg_y),
        (seg, seg_x, 1, seg_x),
        (seg, seg_y, 0, seg_y),
        (seg_x, seg_d, 0, seg_y),
        (seg_y, seg_d, 1, seg_x),
    )

    def outgoing(index):
        sent, _, part, target = plan[index]
        return copy(index, sent, part, target)

    def arrived(index):
        _, got, part, target = plan[index]
        copy(index, got, part, target).wait_recv()

    for start in range(0, row_count, LOC):
        key_value_block(
            start, rows_ref, place_ref, value_src_ref, wk_ref, wv_ref, normed_ref,
            k_ref, v_ref, kv_ref, seg * sparse,
        )
    pl.semaphore_wait(barrier, 2)
    for index in range(4):
        outgoing(index).start()
    q_ref[...] = fold_rows(normed_ref[...], wq_ref[...]).astype(jnp.bfloat16)

    def near_rows(start):
        block = pl.ds(start, LOC)

        @pl.loop(0, RATE)
        def _(phase):
            lanes = pl.ds(pl.multiple_of(phase * LANES, LANES), LANES)
            near_ref[block, lanes] = near_block(
                where_ref[0] - start, q_ref[block, lanes], k_ref[block, lanes], v_ref[block, lanes]
            )

    near_rows(0)
    for index in (0, 1):
        arrived(index)
        outgoing(index + 4).start()
    for start in range(LOC, row_count, LOC):
        near_rows(start)
    for index in range(2, 6):
        arrived(index)
    sum_ref[...] = jnp.zeros_like(sum_ref)

    @pl.loop(0, RATE)
    def _(phase):
        lanes = pl.ds(pl.multiple_of(phase * LANES, LANES), LANES)
        starts = phase_starts(phase, row_count)
        query = jnp.concatenate([q_ref[pl.ds(at, PHASE_ROWS), lanes] for at in starts], axis=0)
        near_own = jnp.concatenate([near_ref[pl.ds(at, PHASE_ROWS), lanes] for at in starts], axis=0)
        packed = kv_ref[:, pl.ds(pl.multiple_of(phase * PACKED, PACKED), PACKED)]
        sum_ref[...] += far_phase(
            phase, where_ref, query, near_own, near_ref[:, lanes], packed,
            value_src_ref[:, lanes], att_ref, starts,
        )

    write_ordered(where_ref, sum_ref, out_ref)
    for index in range(6):
        outgoing(index).wait_send()


def attention(rows, place, query_weight, key_weight, value_weight, valid_limit, row_count):
    seg_count = lax.axis_size("seg")
    seg_here = lax.axis_index("seg")
    seg_tok = seg_count * row_count
    sparse = row_count // RATE
    seg_start = lax.axis_index("grp") * seg_tok
    where = jnp.stack([
        valid_limit - seg_start - seg_here * row_count,
        valid_limit - seg_start,
        seg_here * sparse,
    ]).astype(jnp.int32)
    key_src, value_src = (jnp.asarray(src) for src in lane_sources())
    params = pltpu.CompilerParams(vmem_limit_bytes=VMEM_LIMIT)
    whole = pl.BlockSpec(memory_space=pltpu.VMEM)
    scalars = pl.BlockSpec(memory_space=pltpu.SMEM)
    lane_weights = pl.pallas_call(
        pick_weights_kernel,
        out_shape=(jax.ShapeDtypeStruct((D, RATE * LANES), jnp.bfloat16),) * 3,
        in_specs=[whole] * 5,
        out_specs=(whole,) * 3,
        compiler_params=params,
        cost_estimate=pl.CostEstimate(
            flops=6 * D * D * RATE * LANES, bytes_accessed=14 * D * D, transcendentals=0
        ),
        name="pick_weights",
    )(key_src, value_src, query_weight, key_weight, value_weight)
    lanes = (row_count, RATE * LANES)
    wide = jax.ShapeDtypeStruct(lanes, jnp.bfloat16)
    if (seg_count, lax.axis_size("grp")) == (4, 8):
        return pl.pallas_call(
            attend_kernel,
            out_shape=jax.ShapeDtypeStruct((row_count, D), jnp.bfloat16),
            in_specs=[scalars] + [whole] * 6,
            out_specs=whole,
            scratch_shapes=[
                pltpu.VMEM((row_count, D), jnp.bfloat16),
                pltpu.VMEM(lanes, jnp.bfloat16),
                pltpu.VMEM(lanes, jnp.bfloat16),
                pltpu.VMEM(lanes, jnp.bfloat16),
                pltpu.VMEM((seg_count * sparse, RATE * PACKED), jnp.bfloat16),
                pltpu.VMEM(lanes, jnp.float32),
                pltpu.VMEM((row_count, LANES), jnp.bfloat16),
                pltpu.VMEM((row_count, D), jnp.float32),
                pltpu.SemaphoreType.DMA((6,)),
                pltpu.SemaphoreType.DMA((6,)),
            ],
            compiler_params=pltpu.CompilerParams(
                collective_id=1, has_side_effects=True, vmem_limit_bytes=VMEM_LIMIT
            ),
            name="attend",
        )(where, rows, place, value_src, *lane_weights)
    query, key, value, packed = pl.pallas_call(
        qkv_kernel,
        out_shape=(wide, wide, wide, jax.ShapeDtypeStruct((sparse, RATE * PACKED), jnp.bfloat16)),
        in_specs=[whole] * 6,
        out_specs=(whole,) * 4,
        scratch_shapes=[pltpu.VMEM((row_count, D), jnp.bfloat16)],
        compiler_params=params,
        name="qkv",
    )(rows, place, value_src, *lane_weights)
    shared = lax.all_gather(packed, "seg", axis=0)
    tile = pl.BlockSpec((LOC, LANES), lambda block, phase: (block, phase))
    near = pl.pallas_call(
        near_kernel,
        grid=(row_count // LOC, RATE),
        out_shape=jax.ShapeDtypeStruct((row_count, RATE * LANES), jnp.float32),
        in_specs=[scalars, tile, tile, tile],
        out_specs=tile,
        compiler_params=params,
        cost_estimate=pl.CostEstimate(
            flops=8 * row_count * LOC * HEADS * LANES // 2,
            bytes_accessed=20 * row_count * LANES,
            transcendentals=row_count * LOC * HEADS,
        ),
        name="near",
    )(where, query, key, value)
    tall = pl.BlockSpec((row_count, LANES), lambda phase: (0, phase))
    return pl.pallas_call(
        far_kernel,
        grid=(RATE,),
        out_shape=jax.ShapeDtypeStruct((row_count, D), jnp.bfloat16),
        in_specs=[
            scalars,
            pl.BlockSpec((1, LANES), lambda phase: (0, phase)),
            tall,
            tall,
            pl.BlockSpec((seg_count, sparse, PACKED), lambda phase: (0, 0, phase)),
        ],
        out_specs=pl.BlockSpec((row_count, D), lambda phase: (0, 0)),
        scratch_shapes=[
            pltpu.VMEM((row_count, LANES), jnp.bfloat16),
            pltpu.VMEM((row_count, D), jnp.float32),
        ],
        compiler_params=params,
        name="far",
    )(where, value_src, query, near, shared)


def block_part(ref, rows, part):
    width = ref.shape[1]
    edge = width // 6 // 128 * 128
    first, last = {
        "all": (0, width),
        "left": (0, width // 2),
        "right": (width // 2, width),
        "left_edge": (0, edge),
        "middle": (edge, width - edge),
        "right_edge": (width - edge, width),
    }[part]
    return ref.at[rows, first:last]


def expert_kernel(
    tokens_ref, gate_ref, up_ref, down_ref, proj_ref, slot_ref, out_ref,
    wide_ref, deep_ref, normed_ref, hidden_ref, embedded_ref, send_sem, recv_sem,
):
    seg, grp = lax.axis_index("seg"), lax.axis_index("grp")
    core, z = grp % 2, grp // 2
    seg_x = seg // 2 * 2 + 1 - seg % 2
    seg_y = (seg + 2) % 4
    seg_d = seg_y // 2 * 2 + 1 - seg_y % 2
    sibling = z * 2 + 1 - core
    gathered = (wide_ref, deep_ref)
    depth = (gate_ref.shape[0], down_ref.shape[0])
    copies = {
        "up": (0, (seg, grp + 2), "all", "all"),
        "down": (9, (seg, grp - 2), "all", "all"),
        "x": (1, (seg_x, grp), "all", "all"),
        "y": (2, (seg_y, grp), "all", "all"),
        "xy": (3, (seg_y, grp), "left", "left_edge"),
        "yx": (4, (seg_x, grp), "right", "right_edge"),
        "own": (5, (seg, sibling), "all", "all"),
        "own_x": (6, (seg, sibling), "all", "all"),
        "own_y": (7, (seg, sibling), "all", "all"),
        "own_d": (8, (seg, sibling), "all", "all"),
        "mid_up": (10, (seg, grp + 2), "middle", "middle"),
        "mid_down": (11, (seg, grp - 2), "middle", "middle"),
    }
    sent_block = {
        "up": seg, "down": seg, "x": seg, "y": seg, "xy": seg_x, "yx": seg_y,
        "own": seg, "own_x": seg_x, "own_y": seg_y, "own_d": seg_d,
        "mid_up": seg_d, "mid_down": seg_d,
    }
    got_block = {
        "up": seg, "x": seg_x, "y": seg_y, "xy": seg_d, "yx": seg_d,
        "own": seg, "own_x": seg_x, "own_y": seg_y, "own_d": seg_d,
        "mid_up": seg_d,
    }
    landing = {"down": 0, "mid_up": 9, "mid_down": 9}

    def rows_of(which, block_seg, j, block_core):
        owner = block_seg * 8 + j * 2 + block_core
        return pl.ds(pl.multiple_of(owner * depth[which], 16), depth[which])

    def outgoing(which, j, kind, home=False):
        index, target, *parts = copies[kind]
        rows = rows_of(which, sent_block[kind], j, core)
        block = block_part(gathered[which], rows, parts[0 if home else 1])
        return pltpu.make_async_remote_copy(
            src_ref=block,
            dst_ref=block,
            send_sem=send_sem.at[which, j, index],
            recv_sem=recv_sem.at[which, j, landing.get(kind, index)],
            device_id=target,
            device_id_type=pl.DeviceIdType.MESH,
        )

    def arrived(which, j, kind, home=False):
        index, _, *parts = copies[kind]
        from_core = 1 - core if kind.startswith("own") else core
        rows = rows_of(which, got_block[kind], j, from_core)
        block = block_part(gathered[which], rows, parts[0 if home else 1])
        pltpu.make_async_remote_copy(
            src_ref=block,
            dst_ref=block,
            send_sem=send_sem.at[which, j, index],
            recv_sem=recv_sem.at[which, j, landing.get(kind, index)],
            device_id=(seg, sibling),
            device_id_type=pl.DeviceIdType.MESH,
        ).wait_recv()

    def each_of_wave(k, do):
        if k == 0:
            do(z, True, True)
        else:
            pl.when(z >= k)(lambda: do(z - k, True, False))
            pl.when(z + k <= 3)(lambda: do(z + k, False, True))

    def enter(which, k):
        def do(j, rising, falling):
            if k > 0:
                arrived(which, j, "up")
            if rising:
                pl.when(z < 3)(lambda: outgoing(which, j, "up").start())
            if falling:
                pl.when(z > 0)(lambda: outgoing(which, j, "down").start())
            for kind in ("x", "y", "own"):
                outgoing(which, j, kind).start()
        each_of_wave(k, do)

    def cross(which, k):
        def do(j, rising, falling):
            arrived(which, j, "x")
            outgoing(which, j, "xy", k == 0).start()
            outgoing(which, j, "own_x").start()
            arrived(which, j, "y")
            outgoing(which, j, "yx", k == 0).start()
            outgoing(which, j, "own_y").start()
        each_of_wave(k, do)

    def close(which, k):
        def do(j, rising, falling):
            arrived(which, j, "xy", k == 0)
            arrived(which, j, "yx", k == 0)
            if k > 0:
                arrived(which, j, "mid_up")
            if rising:
                pl.when(z < 3)(lambda: outgoing(which, j, "mid_up").start())
            if falling:
                pl.when(z > 0)(lambda: outgoing(which, j, "mid_down").start())
            outgoing(which, j, "own_d").start()
        each_of_wave(k, do)

    def advance(which, step):
        if 0 <= step < 4:
            enter(which, step)
        if 0 <= step - 1 < 4:
            cross(which, step - 1)
        if 0 <= step - 2 < 4:
            close(which, step - 2)

    def from_sibling(which):
        for j in range(4):
            for kind in ("own", "own_x", "own_y", "own_d"):
                arrived(which, j, kind)

    barrier = pltpu.get_barrier_semaphore()

    def greet(target):
        pl.semaphore_signal(
            barrier, inc=1, device_id=target, device_id_type=pl.DeviceIdType.MESH
        )

    for target in ((seg_x, grp), (seg_y, grp), (seg, sibling)):
        greet(target)
    pl.when(z < 3)(lambda: greet((seg, grp + 2)))
    pl.when(z > 0)(lambda: greet((seg, grp - 2)))
    pl.semaphore_wait(barrier, 4 + (z + 1) // 2 % 2)

    half_width = gate_ref.shape[1]
    wide_ref[rows_of(0, seg, z, core), :half_width] = gate_ref[...]
    wide_ref[rows_of(0, seg, z, core), half_width:] = up_ref[...]
    deep_ref[rows_of(1, seg, z, core), :] = down_ref[...]
    advance(0, 0)

    row_count = tokens_ref.shape[0]

    @pl.loop(0, row_count // ROW_TILE)
    def _(tile):
        rows = pl.ds(pl.multiple_of(tile * ROW_TILE, ROW_TILE), ROW_TILE)
        normed_ref[rows, :] = layer_norm(
            tokens_ref[rows, :].astype(jnp.float32), 1e-06
        ).astype(jnp.bfloat16)

    for step in range(1, 6):
        advance(0, step)
        advance(1, step - 3)
    from_sibling(0)

    def gate_up(tile):
        rows = pl.ds(tile * ROW_TILE, ROW_TILE)

        @pl.loop(0, half_width // COLUMN_TILE)
        def _(part):
            at = pl.multiple_of(part * COLUMN_TILE, COLUMN_TILE)
            past = pl.multiple_of(part * COLUMN_TILE + half_width, COLUMN_TILE)
            normed = normed_ref[rows, :]
            gate = fold_rows(normed, wide_ref[:, pl.ds(at, COLUMN_TILE)])
            up = fold_rows(normed, wide_ref[:, pl.ds(past, COLUMN_TILE)])
            hidden_ref[rows, pl.ds(at, COLUMN_TILE)] = (
                gate / (1.0 + jnp.exp(-gate)) * up
            ).astype(jnp.bfloat16)

    tiles = row_count // ROW_TILE
    gate_up(0)
    for step in range(6, 9):
        advance(1, step - 3)
        if step - 5 < tiles:
            gate_up(step - 5)
    for tile in range(4, tiles):
        gate_up(tile)
    from_sibling(1)

    @pl.loop(0, tiles)
    def _(tile):
        rows = pl.ds(pl.multiple_of(tile * ROW_TILE, ROW_TILE), ROW_TILE)
        mixed = tokens_ref[rows, :].astype(jnp.float32) + fold_rows(
            hidden_ref[rows, :], deep_ref[...]
        )
        final = layer_norm(mixed, 1e-06).astype(jnp.bfloat16)
        embedded_ref[rows, :] = fold_rows(final, proj_ref[...]).astype(jnp.bfloat16)

    @pl.loop(0, out_ref.shape[0] // ROW_TILE)
    def _(tile):
        start = pl.multiple_of(tile * ROW_TILE, ROW_TILE)
        slot = lax.broadcasted_iota(jnp.int32, (ROW_TILE, row_count), 0) + start
        pick = (slot == slot_ref[...]).astype(jnp.bfloat16)
        out_ref[pl.ds(start, ROW_TILE), :] = fold_rows(pick, embedded_ref[...]).astype(jnp.bfloat16)

    for which in range(2):
        for j in range(4):
            for kind in copies:
                if kind in ("up", "mid_up"):
                    pl.when((z < 3) & (z >= j))(lambda: outgoing(which, j, kind).wait_send())
                elif kind in ("down", "mid_down"):
                    pl.when((z > 0) & (z <= j))(lambda: outgoing(which, j, kind).wait_send())
                elif kind in ("xy", "yx"):
                    pl.when(z == j)(lambda: outgoing(which, j, kind, True).wait_send())
                    pl.when(z != j)(lambda: outgoing(which, j, kind).wait_send())
                else:
                    outgoing(which, j, kind).wait_send()


def gathered_send_rows(
    tile_tokens, gate_weight, up_weight, down_weight, proj_weight, slot_index, slots
):
    row_count, width = tile_tokens.shape
    hidden_width = gate_weight.shape[1]
    whole = pl.BlockSpec(memory_space=pltpu.VMEM)
    return pl.pallas_call(
        expert_kernel,
        out_shape=jax.ShapeDtypeStruct((slots, D), jnp.bfloat16),
        in_specs=[whole] * 6,
        out_specs=whole,
        scratch_shapes=[
            pltpu.VMEM((width, 2 * hidden_width), jnp.bfloat16),
            pltpu.VMEM((hidden_width, width), jnp.bfloat16),
            pltpu.VMEM((row_count, width), jnp.bfloat16),
            pltpu.VMEM((row_count, hidden_width), jnp.bfloat16),
            pltpu.VMEM((row_count, D), jnp.bfloat16),
            pltpu.SemaphoreType.DMA((2, 4, 12)),
            pltpu.SemaphoreType.DMA((2, 4, 10)),
        ],
        compiler_params=pltpu.CompilerParams(
            collective_id=0, has_side_effects=True, vmem_limit_bytes=VMEM_LIMIT
        ),
        name="feed_forward",
    )(tile_tokens, gate_weight, up_weight, down_weight, proj_weight, slot_index.reshape(1, -1))


def feed_forward(tile_tokens, gate_weight, up_weight, down_weight, proj_weight):
    residual = tile_tokens.astype(jnp.float32)
    normed = layer_norm(residual, 1e-06).astype(jnp.bfloat16)
    gate_acc = fold_rows(normed, lax.all_gather(gate_weight, ("seg", "grp"), axis=0, tiled=True))
    up_acc = fold_rows(normed, lax.all_gather(up_weight, ("seg", "grp"), axis=0, tiled=True))
    hidden = (jax.nn.silu(gate_acc) * up_acc).astype(jnp.bfloat16)
    mixed = fold_rows(hidden, lax.all_gather(down_weight, ("seg", "grp"), axis=0, tiled=True))
    final_normed = layer_norm(residual + mixed, 1e-06).astype(jnp.bfloat16)
    return fold_rows(final_normed, proj_weight).astype(jnp.bfloat16)


def shards(
    tile_tokens,
    gate_weight,
    up_weight,
    down_weight,
    proj_weight,
    query_weight,
    key_weight,
    value_weight,
    tile_rank,
    valid_count,
):
    seg_count = lax.axis_size("seg")
    grp_count = lax.axis_size("grp")
    devices = seg_count * grp_count
    row_count = tile_tokens.shape[0]
    slot_cap = 2 * row_count // devices
    slots = devices * slot_cap
    seg_tok = seg_count * row_count
    target_grp = tile_rank // seg_tok
    target_seg = tile_rank % seg_tok // row_count
    target = target_seg * grp_count + target_grp
    onehot = target[:, None] == jnp.arange(devices, dtype=jnp.int32)[None, :]
    order = jnp.arange(row_count, dtype=jnp.int32)
    earlier = (order[None, :] < order[:, None]).astype(jnp.bfloat16)
    before = fold_rows(earlier, onehot.astype(jnp.bfloat16))
    rank_within = jnp.sum(jnp.where(onehot, before, 0.0), axis=1).astype(jnp.int32)
    slot_index = target * slot_cap + rank_within
    filled = jnp.arange(slots, dtype=jnp.int32)[:, None] == slot_index[None, :]
    all_ranks = lax.all_gather(tile_rank, ("seg", "grp"), axis=0)
    if (seg_count, grp_count) == (4, 8):
        send_rows = gathered_send_rows(
            tile_tokens, gate_weight, up_weight, down_weight, proj_weight, slot_index, slots
        )
    else:
        embedded = feed_forward(tile_tokens, gate_weight, up_weight, down_weight, proj_weight)
        send_rows = fold_rows(filled.astype(jnp.bfloat16), embedded).astype(jnp.bfloat16)
    all_ranks, send_rows, query_weight, key_weight, value_weight = lax.optimization_barrier(
        (all_ranks, send_rows, query_weight, key_weight, value_weight)
    )
    within = all_ranks - lax.axis_index("grp") * seg_tok - lax.axis_index("seg") * row_count
    mine = (within >= 0) & (within < row_count)
    mine_before = lax.dot_general(
        mine.astype(jnp.bfloat16),
        earlier,
        (((1,), (1,)), ((), ())),
        preferred_element_type=jnp.float32,
    ).astype(jnp.int32)
    row = within // LOC * LOC + within % RATE * PHASE_ROWS + within % LOC // RATE
    got_slot = jnp.where(mine, mine_before, -1)[:, None, :]
    here = got_slot == jnp.arange(slot_cap, dtype=jnp.int32)[None, :, None]
    got_place = (jnp.sum(jnp.where(here, row[:, None, :] + 1, 0), axis=2) - 1).reshape(1, slots)
    got_rows = lax.all_to_all(
        send_rows.reshape(devices, slot_cap, D),
        ("seg", "grp"),
        split_axis=0,
        concat_axis=0,
        tiled=True,
    ).reshape(slots, D)
    attended = attention(
        got_rows, got_place, query_weight, key_weight, value_weight, valid_count[0], row_count
    )
    return attended[None]


def solution(mesh):
    return jax.shard_map(
        shards,
        mesh=mesh,
        in_specs=(
            P(("seg", "grp"), None),
            P(("seg", "grp"), None),
            P(("seg", "grp"), None),
            P(("seg", "grp"), None),
            P(),
            P(),
            P(),
            P(),
            P(("seg", "grp")),
            P(),
        ),
        out_specs=P("grp", "seg", None),
        check_vma=False,
    )
```
